256 devices in a mesh: dp: 8 (over x_lo, y), slab: 32 (over x_hi, z, core).
Axes of the slice: x: 4 (x_hi: 2, x_lo: 2; x = x_hi * 2 + x_lo), y: 4, z: 8, core: 2. Of those that a mesh axis runs over, the one named last changes fastest.
Arguments:
- field: bfloat16 [8, 64, 64, 4096], P('dp', 'slab'), may hold values from -6 to 6
- cotangent: bfloat16 [8, 64, 64, 4096], P('dp', 'slab'), may hold values from -6 to 6
- mode_weights: bfloat16 [256, 16, 64, 128], P('slab'), may hold values from -5 to 5
- w_local: bfloat16 [64, 64], replicated, may hold values from -0.75 to 0.75
- bias: float32 [64], replicated, may hold values from -4 to 4
Outputs:
- grad_field: bfloat16 [8, 64, 64, 4096], P('dp', 'slab')
- grad_modes: float32 [256, 16, 64, 128], P('slab')
The draws below stay inside these ranges and needn't reach their ends.
All inputs are finite; a program needn't handle non-finite values.
Results may differ from the reference program's by a relative error of at most 0.005.
Values sent between devices are 32-bit elements; how exact they have to be, the bound alone decides.
No kernel may reach another device: no remote copies, remote signals or barrier semaphores. Data moves between devices by JAX's collectives and lax.ppermute only.
A program may use at most 128 MiB of HBM per device.

```python
import math
import jax
import jax.numpy as jnp
from jax import lax

C = 64
KX = 16
KY = 16
KT = 16
NY = 64
NT = 64
CX = 2
NX = 64
BATCH = 8
KYT = 256
N_SLAB = 32


def levels(own_key, extent, cuts, low, top_value):
    factor_of, own = 1.0, jax.random.fold_in(own_key, 6)
    for axis_at, parts in cuts:
        heights = jnp.exp(jax.random.uniform(jax.random.fold_in(own, axis_at), (parts,), jnp.float32, low / len(cuts), top_value / len(cuts)))
        factor_of = factor_of * jnp.repeat(heights, extent[axis_at] // parts).reshape([-1 if axis == axis_at else 1 for axis in range(len(extent))])
    return factor_of


def centred(key, extent, width, reach, pieces=(), kind=jnp.bfloat16):
    array = jax.random.normal(key, extent, jnp.float32) * width
    if len(pieces) > 0:
        array = levels(key, extent, pieces, -0.22, 0.18) * array
    return jnp.clip(array, min=-reach, max=reach).astype(kind)


def setup_inputs(seed: int = 0) -> dict:
    key_of = jax.random.split(jax.random.key(seed), 6)
    field = centred(key_of[0], (BATCH, NX, NY, NT * C), 1.0, 6.0, ((0, 8), (1, 32)))
    cotangent = centred(key_of[1], (BATCH, NX, NY, NT * C), 1.0, 6.0, ((0, 8), (1, 32)))
    mode_weights = centred(key_of[2], (KYT, KX, C, 2 * C), (0.5 * (CX * N_SLAB * NY * NT) ** 0.5 * (KX * KY * KT * 2 * C) ** -0.5), 5.0, ((0, 32),))
    w_local = centred(key_of[3], (C, C), C ** -0.5, 0.75)
    bias = centred(key_of[4], (C,), 1.0, 4.0, (), jnp.float32)
    return {"field": field, "cotangent": cotangent, "mode_weights": mode_weights, "w_local": w_local, "bias": bias}


HIGHEST = lax.Precision.HIGHEST
SQRT_TWO_PI = math.sqrt(2.0 / math.pi)

def signed_freqs(count):
    index = jnp.arange(count, dtype=jnp.int32)
    return jnp.where(index < count // 2, index, index - count)

def trig_tables(freqs, positions, length):
    phase = (freqs[:, None] * positions[None, :] % length).astype(jnp.float32) * (2.0 * math.pi / length)
    factor = 1.0 / math.sqrt(length)
    return (jnp.cos(phase) * factor, jnp.sin(phase) * factor)

def time_table(modes, length):
    cosine, sine = trig_tables(jnp.arange(modes, dtype=jnp.int32), jnp.arange(length, dtype=jnp.int32), length)
    return jnp.concatenate([cosine, -sine], 0).T

def y_analysis(first, cosine, sine, modes):
    real_in = first[:, :, :, :modes]
    imag_in = first[:, :, :, modes:]

    def applied(table, data):
        return jnp.einsum('ky,bxytc->ktbxc', table, data, precision=HIGHEST)
    real_out = applied(cosine, real_in) + applied(sine, imag_in)
    imag_out = applied(cosine, imag_in) - applied(sine, real_in)
    joined = jnp.concatenate([real_out, imag_out], -1)
    return joined.reshape((-1,) + joined.shape[2:])

def x_analysis(data, cosine, sine):
    half = data.shape[-1] // 2
    real_in = data[..., :half]
    imag_in = data[..., half:]

    def applied(table, part_in):
        return jnp.einsum('kx,mbxc->mbkc', table, part_in, precision=HIGHEST)
    real_out = applied(cosine, real_in) + applied(sine, imag_in)
    imag_out = applied(cosine, imag_in) - applied(sine, real_in)
    return jnp.concatenate([real_out, imag_out], -1)

def x_synthesis(data, cosine, sine):
    half = data.shape[-1] // 2
    real_in = data[..., :half]
    imag_in = data[..., half:]

    def applied(table, part_in):
        return jnp.einsum('kx,mbkc->mbxc', table, part_in, precision=HIGHEST)
    real_out = applied(cosine, real_in) - applied(sine, imag_in)
    imag_out = applied(cosine, imag_in) + applied(sine, real_in)
    return jnp.concatenate([real_out, imag_out], -1)

def y_synthesis(data, cosine, sine, modes):
    half = data.shape[-1] // 2
    shaped = data.reshape((cosine.shape[0], modes) + data.shape[1:])
    real_in = shaped[..., :half]
    imag_in = shaped[..., half:]

    def applied(table, part_in):
        return jnp.einsum('ky,ktbxc->bxytc', table, part_in, precision=HIGHEST)
    real_out = applied(cosine, real_in) - applied(sine, imag_in)
    imag_out = applied(cosine, imag_in) + applied(sine, real_in)
    return jnp.concatenate([real_out, imag_out], 3)

def t_synthesis(data, table):
    return jnp.einsum('bxykc,tk->bxytc', data, table, precision=HIGHEST)

def split_parts(data):
    half = data.shape[-1] // 2
    return (data[..., :half], data[..., half:])

def mix_modes(spectra, weights):
    w_real, w_imag = split_parts(weights.astype(jnp.float32))
    s_real, s_imag = split_parts(spectra)

    def applied(left, right):
        return jnp.einsum('mbki,mkio->mbko', left, right, precision=HIGHEST)
    real_out = applied(s_real, w_real) - applied(s_imag, w_imag)
    imag_out = applied(s_real, w_imag) + applied(s_imag, w_real)
    return jnp.concatenate([real_out, imag_out], -1)

def weight_grads(spectra, grads):
    s_real, s_imag = split_parts(spectra)
    g_real, g_imag = split_parts(grads)

    def applied(left, right):
        return jnp.einsum('mbki,mbko->mkio', left, right, precision=HIGHEST)
    real_out = applied(s_real, g_real) + applied(s_imag, g_imag)
    imag_out = applied(s_real, g_imag) - applied(s_imag, g_real)
    return jnp.concatenate([real_out, imag_out], -1)

def adjoint_modes(grads, weights):
    w_real, w_imag = split_parts(weights.astype(jnp.float32))
    g_real, g_imag = split_parts(grads)

    def applied(left, right):
        return jnp.einsum('mkio,mbko->mbki', left, right, precision=HIGHEST)
    real_out = applied(w_real, g_real) + applied(w_imag, g_imag)
    imag_out = applied(w_real, g_imag) - applied(w_imag, g_real)
    return jnp.concatenate([real_out, imag_out], -1)

def gelu_slope(values):
    inner = SQRT_TWO_PI * (values + 0.044715 * values ** 3)
    tanh_value = jnp.tanh(inner)
    return 0.5 * (1.0 + tanh_value) + 0.5 * values * (1.0 - tanh_value * tanh_value) * SQRT_TWO_PI * (1.0 + 3.0 * 0.044715 * values * values)

def reference(field, cotangent, mode_weights, w_local, bias):
    t_table = time_table(KT, NT)
    t_narrow = t_table.astype(jnp.bfloat16)
    y_cos, y_sin = trig_tables(signed_freqs(KY), jnp.arange(NY, dtype=jnp.int32), NY)
    x_cos, x_sin = trig_tables(signed_freqs(KX), jnp.arange(NX, dtype=jnp.int32), NX)

    def analyse(values):
        first = jnp.einsum('rtc,tk->rkc', values.reshape(-1, NT, C).astype(jnp.float32), t_narrow.astype(jnp.float32), precision=HIGHEST)
        second = y_analysis(first.reshape(1, NX, NY, 2 * KT, C), y_cos, y_sin, KT)
        return x_analysis(second, x_cos, x_sin)

    def synthesise(spectra):
        rows_back = x_synthesis(spectra, x_cos, x_sin)
        return t_synthesis(y_synthesis(rows_back, y_cos, y_sin, KT), t_table)

    def per_sample(carry, pair):
        sample, cot_sample = pair
        sample = sample[None]
        spectra = analyse(sample)
        spec = synthesise(mix_modes(spectra, mode_weights))
        flat = sample.reshape(-1, C)
        pre_act = spec.reshape(-1, C) + jnp.dot(flat, w_local, preferred_element_type=jnp.float32) + bias
        grad_pre = (cot_sample.reshape(-1, C).astype(jnp.float32) * gelu_slope(pre_act)).astype(jnp.bfloat16)
        grad_spectra = analyse(grad_pre.reshape(sample.shape))
        carry = carry + weight_grads(spectra, grad_spectra)
        back = synthesise(adjoint_modes(grad_spectra, mode_weights))
        grad_rows = back.reshape(-1, C) + jnp.dot(grad_pre, w_local.T, preferred_element_type=jnp.float32)
        return (carry, grad_rows.astype(jnp.bfloat16).reshape(sample.shape[1:]))
    total, grads = lax.scan(per_sample, jnp.zeros(mode_weights.shape, jnp.float32), (field, cotangent))
    return (grads, total)
```

```python
import math

import jax
import jax.numpy as jnp
import ml_dtypes
import numpy as np
from jax import lax
from jax.experimental import pallas as pl
from jax.experimental.pallas import tpu as pltpu
from jax.sharding import PartitionSpec as P

C = 64
K = 16
N = 64
CX = 2
SLABS = 32
DP = 8
TP = N // 2

BF = jnp.bfloat16
F32 = jnp.float32
SQRT_TWO_PI = math.sqrt(2.0 / math.pi)


def trig(freqs):
    phase = (freqs[:, None] * np.arange(N)[None, :] % N) * (2.0 * math.pi / N)
    return np.cos(phase) / math.sqrt(N), np.sin(phase) / math.sqrt(N)


def rounded(table):
    return table.astype(np.float32).astype(ml_dtypes.bfloat16)


def wide(table):
    high = rounded(table)
    low = rounded(table - high.astype(np.float64))
    return np.concatenate([high, low, high], 1)


def twice_table(table):
    high = rounded(table)
    low = rounded(table - high.astype(np.float64))
    return np.concatenate([high, low], 1)


SIGNED = np.concatenate([np.arange(K // 2), np.arange(-K // 2, 0)])
COS, SIN = trig(SIGNED)
T_COS, T_SIN = trig(np.arange(K))
P_RE, P_IM = T_COS.T, -T_SIN.T

Y_IN = twice_table(np.stack([COS, SIN], 1).reshape(2 * K, N))
Y_OUT = wide(np.concatenate([COS, SIN], 0).T)
X_IN = wide(np.concatenate([COS, SIN], 0))
X_OUT = wide(np.concatenate([COS, SIN], 0).T)


def t_in():
    re = rounded(P_RE).astype(np.float64).reshape(TP, 2, K)
    im = rounded(P_IM).astype(np.float64).reshape(TP, 2, K)
    rows_re = np.concatenate([re, im], 0)
    rows_im = np.concatenate([im, -re], 0)
    both = np.stack([rows_re, rows_im], 0)
    table = both.transpose(0, 2, 3, 1).reshape(4 * K, 2 * TP)
    return rounded(np.concatenate([table, table], 1))


def t_out():
    re = P_RE.reshape(TP, 2, K)
    im = P_IM.reshape(TP, 2, K)
    of_c = np.stack([re, im], 2)
    of_s = np.stack([im, -re], 2)
    return wide(np.concatenate([of_c, of_s], 0).reshape(2 * TP, 4 * K))


TABLES = {
    "y_in": Y_IN,
    "t_in": t_in(),
    "y_out": Y_OUT,
    "x_in": X_IN,
    "x_out": X_OUT,
    "t_out": t_out(),
}
PLACES = {}
for name, values in TABLES.items():
    PLACES[name] = (sum(TABLES[other].shape[0] for other in PLACES), *values.shape)
PACKED = np.concatenate([np.pad(v, ((0, 0), (0, 256 - v.shape[1]))) for v in TABLES.values()], 0)


def table(ref, name):
    first, rows, columns = PLACES[name]
    return ref[first : first + rows, :columns]


def dot(left, right):
    return jnp.dot(left, right, preferred_element_type=F32)


def split(data):
    high = data.astype(BF)
    return high, (data - high.astype(F32)).astype(BF)


def stack3(data):
    high, low = split(data)
    return jnp.concatenate([high, high, low], 0)


def stack2(data):
    high, low = split(data)
    return jnp.concatenate([high, low], 0)


def low_lanes(shape):
    return lax.broadcasted_iota(jnp.int32, shape, 1) < C


def swap(data):
    return pltpu.roll(data, C, 1)


def turned(data):
    other = swap(data)
    return jnp.where(low_lanes(data.shape), -other, other)


def lanes(blocks):
    return jnp.concatenate(blocks, 1)


Y_TILES = 8


def y_analysis_store(chunk, first_tile, tiles, y_in, scratch):
    out = dot(y_in, jnp.concatenate([chunk, chunk], 0))
    for j in range(tiles):
        scratch[pl.ds(first_tile + j, 2 * K, stride=TP), :] = out[:, j * 128 : (j + 1) * 128]


def t_analysis(scratch, t_table, out_ref, x, group=4):
    low = low_lanes((K, 128))
    for first in range(0, K, group):
        data = lanes([scratch[(first + j) * 2 * TP : (first + j + 1) * 2 * TP, :] for j in range(group)])
        res = dot(t_table, stack2(data))
        for j in range(group):
            re0, re1, im0, im1 = (res[q * K : (q + 1) * K, j * 128 : (j + 1) * 128] for q in range(4))
            both = jnp.where(low, re0, im1) + swap(jnp.where(low, im0, re1))
            out_ref[2 * (first + j), x] = both[:8]
            out_ref[2 * (first + j) + 1, x] = both[8:]


def t_synthesis(w_ref, t_table, scratch, x, group=4):
    low = low_lanes((K, 128))
    zero = jnp.zeros((K, 128), F32)
    for first in range(0, K, group):
        blocks = []
        for j in range(group):
            w = jnp.concatenate([w_ref[2 * (first + j), x], w_ref[2 * (first + j) + 1, x]], 0)
            other = swap(w)
            blocks.append(
                jnp.concatenate(
                    [
                        jnp.where(low, w, zero),
                        jnp.where(low, other, zero),
                        jnp.where(low, zero, other),
                        jnp.where(low, zero, w),
                    ],
                    0,
                )
            )
        res = dot(t_table, stack3(lanes(blocks)))
        for j in range(group):
            for cs in range(2):
                scratch[pl.ds(cs * K + first + j, TP, stride=2 * K), :] = res[
                    cs * TP : (cs + 1) * TP, j * 128 : (j + 1) * 128
                ]


def y_synthesis(scratch, first_tile, tiles, y_out):
    data = lanes(
        [
            scratch[pl.ds(pl.multiple_of((first_tile + j) * 2 * K, 2 * K), 2 * K), :]
            for j in range(tiles)
        ]
    )
    return dot(y_out, stack3(data))


def channel_map(chunk, weight, tiles, contracted=0):
    rows = jnp.concatenate([chunk[:, j * 128 : (j + 1) * 128] for j in range(tiles)], 0)
    out = lax.dot_general(
        rows, weight, (((1,), (contracted,)), ((), ())), preferred_element_type=F32
    )
    return lanes([out[j * N : (j + 1) * N] for j in range(tiles)])


def lane_slice(step, tiles):
    return pl.ds(pl.multiple_of(step * tiles * 128, tiles * 128), tiles * 128)


def analyse_kernel(
    field_in, cot_in, w_in, tables_in, map_in, bias_in,
    out_ref, field_ref, cot_ref, w_ref, tables_ref, map_ref, bias_ref,
    scratch, small_map, small_bias, sems,
):
    copies = [
        pltpu.make_async_copy(source, target, sems.at[i])
        for i, (source, target) in enumerate(
            [
                (tables_in, tables_ref),
                (field_in.at[0], field_ref.at[0]),
                (field_in.at[1], field_ref.at[1]),
                (map_in, small_map),
                (bias_in, small_bias),
                (w_in, w_ref),
                (cot_in, cot_ref),
            ]
        )
    ]
    for copy in copies:
        copy.start()
    copies[0].wait()
    y_in, t_table = table(tables_ref, "y_in"), table(tables_ref, "t_in")
    for x in range(CX):
        copies[1 + x].wait()

        @pl.loop(0, TP // Y_TILES)
        def _(step):
            y_analysis_store(
                field_ref[x, :, lane_slice(step, Y_TILES)], step * Y_TILES, Y_TILES, y_in, scratch
            )

        t_analysis(scratch, t_table, out_ref, x)
    copies[3].wait()
    copies[4].wait()
    wide_map = jnp.concatenate([small_map[...]] * 2, 1)
    wide_map = jnp.concatenate([wide_map] * 2, 0)
    row = lax.broadcasted_iota(jnp.int32, (2 * C, 2 * C), 0) // C
    lane = lax.broadcasted_iota(jnp.int32, (2 * C, 2 * C), 1) // C
    map_ref[...] = jnp.where(row == lane, wide_map, jnp.zeros_like(wide_map))
    bias_ref[...] = jnp.concatenate([small_bias[...]] * 2, 1)
    copies[5].wait()
    copies[6].wait()


def gelu_slope(z):
    inner = SQRT_TWO_PI * (z + 0.044715 * z * z * z)
    tanh_value = jnp.tanh(inner)
    return 0.5 * (1.0 + tanh_value) + 0.5 * z * (1.0 - tanh_value * tanh_value) * SQRT_TWO_PI * (
        1.0 + 3.0 * 0.044715 * z * z
    )


def middle_kernel(w_ref, field_ref, cot_ref, map_ref, bias_ref, tables_ref, gz_ref, out_ref, syn, ana):
    y_in, y_out, t_in, t_out = (table(tables_ref, name) for name in ("y_in", "y_out", "t_in", "t_out"))

    @pl.loop(0, CX)
    def _(x):
        t_synthesis(w_ref, t_out, syn, x)

        @pl.loop(0, TP // Y_TILES)
        def _(step):
            at = lane_slice(step, Y_TILES)
            spec = y_synthesis(syn, step * Y_TILES, Y_TILES, y_out)
            z = spec + channel_map(field_ref[x, :, at], map_ref[...], Y_TILES) + lanes([bias_ref[...]] * Y_TILES)
            gz = (cot_ref[x, :, at].astype(F32) * gelu_slope(z)).astype(BF)
            gz_ref[x, :, at] = gz
            y_analysis_store(gz, step * Y_TILES, Y_TILES, y_in, ana)

        t_analysis(ana, t_in, out_ref, x)


def final_kernel(w_ref, gz_ref, map_ref, tables_ref, out_ref, syn):
    y_out, t_out = table(tables_ref, "y_out"), table(tables_ref, "t_out")

    @pl.loop(0, CX)
    def _(x):
        t_synthesis(w_ref, t_out, syn, x)

        @pl.loop(0, TP // Y_TILES)
        def _(step):
            at = lane_slice(step, Y_TILES)
            spec = y_synthesis(syn, step * Y_TILES, Y_TILES, y_out)
            out_ref[x, :, at] = (spec + channel_map(gz_ref[x, :, at], map_ref[...], Y_TILES, 1)).astype(BF)


M = 8


def x_analysis(in_ref, x_in):
    data = lanes([in_ref[pl.ds(m, N, stride=M), :] for m in range(M)])
    res = dot(x_in, stack3(data))
    out = []
    for m in range(M):
        cos_part = res[:K, m * 128 : (m + 1) * 128]
        sin_part = res[K:, m * 128 : (m + 1) * 128]
        out.append(cos_part - turned(sin_part))
    return out


def x_synthesis(blocks, x_out, out_ref):
    data = lanes([jnp.concatenate([v, turned(v)], 0) for v in blocks])
    res = dot(x_out, stack3(data))
    for m in range(M):
        out_ref[pl.ds(m, N, stride=M), :] = res[:, m * 128 : (m + 1) * 128]


def mix(u, weights):
    low = low_lanes((K, 128))
    other = swap(u)
    rows = jnp.concatenate([jnp.where(low, u, other), jnp.where(low, other, u)], 0)
    parts = jnp.concatenate(split(rows), 0).astype(F32)
    row = lax.broadcasted_iota(jnp.int32, (4 * K, 128), 0) % K
    half = lax.broadcasted_iota(jnp.int32, (4 * K, 128), 1) // C
    left = lanes([jnp.where(row == 2 * j + half, parts, 0.0).astype(BF) for j in range(K // 2)])
    res = dot(left, weights)
    res = res[: 2 * K] + res[2 * K :]
    return res[:K] + turned(res[K:])


def mix_adjoint(g, weights):
    rows = jnp.concatenate([g, -turned(g)], 0)
    parts = jnp.concatenate(split(rows), 0)
    res = lax.dot_general(parts, weights, (((1,), (1,)), ((), ())), preferred_element_type=F32)
    res = res[: 2 * K] + res[2 * K :]
    row = lax.broadcasted_iota(jnp.int32, (2 * K, 128), 0) % K
    half = lax.broadcasted_iota(jnp.int32, (2 * K, 128), 1) // C
    total = jnp.zeros((2 * K, 128), F32)
    for j in range(K // 2):
        total = total + jnp.where(row == 2 * j + half, res[:, j * 128 : (j + 1) * 128], 0.0)
    total = total + swap(total)
    return jnp.where(low_lanes((K, 128)), total[:K], total[K:])


def spectral_kernel(adjoint, in_ref, w_ref, tables_ref, hat_ref, out_ref):
    spectra = x_analysis(in_ref, table(tables_ref, "x_in"))
    mixed = []
    for m in range(M):
        hat_ref[m] = spectra[m]
        weights = w_ref[m]
        mixed.append(mix_adjoint(spectra[m], weights) if adjoint else mix(spectra[m], weights))
    x_synthesis(mixed, table(tables_ref, "x_out"), out_ref)


G_MODES = 2


def grads_kernel(u_near, u_far, g_near, g_far, out_ref):
    own = lax.broadcasted_iota(jnp.int32, (C, 2 * DP * K), 1) % K
    for j in range(G_MODES):
        m = pl.program_id(0) * G_MODES + j
        u = jnp.concatenate([ref[b, m] for ref in (u_near, u_far) for b in range(DP // 2)], 0)
        g = jnp.concatenate([ref[b, m] for ref in (g_near, g_far) for b in range(DP // 2)], 0)
        u_t = u.T.astype(BF)
        left = lanes([u_t[:C], u_t[C:]])
        right = jnp.concatenate([g, -turned(g)], 0).astype(BF)
        tall = jnp.concatenate([jnp.where(own == kx, left, jnp.zeros_like(left)) for kx in range(K)], 0)
        out_ref[j] = dot(tall, right).reshape(K, C, 2 * C)


PARAMS = pltpu.CompilerParams(vmem_limit_bytes=32 * 1024 * 1024)
IN_VMEM = pl.BlockSpec(memory_space=pltpu.VMEM)
IN_HBM = pl.BlockSpec(memory_space=pltpu.HBM)


def vmem_call(kernel, name, out_shapes, scratch, *operands, specs=None):
    return pl.pallas_call(
        kernel,
        name=name,
        out_shape=out_shapes,
        in_specs=specs or [IN_VMEM] * len(operands),
        out_specs=jax.tree.map(lambda _: IN_VMEM, out_shapes),
        scratch_shapes=scratch,
        compiler_params=PARAMS,
    )(*operands)


def shape(dims, kind=F32):
    return jax.ShapeDtypeStruct(dims, kind)


SPECTRA = shape((SLABS, CX, M, 128))
ROWS = pltpu.VMEM((TP * 2 * K, 128), F32)
Y_RING = 4


def exchange(data):
    return lax.all_to_all(data, "slab", 0, 0, tiled=True)


def gather_samples(data):
    def moved(by):
        return lax.ppermute(
            data, "dp", [(i, i // Y_RING * Y_RING + (i + by) % Y_RING) for i in range(DP)]
        )

    near = jnp.stack([data, moved(1), moved(3), moved(2)], 0)
    return near, lax.ppermute(near, "dp", [(i, (i + Y_RING) % DP) for i in range(DP)])


def body(field, cotangent, mode_weights, w_local, bias):
    grid_shape = (CX, N, N * C)

    def spectral(adjoint, data):
        return vmem_call(
            lambda *refs: spectral_kernel(adjoint, *refs),
            "adjoint" if adjoint else "mix",
            (shape((M, K, 128)), shape((N * M, 128))),
            [],
            data.reshape(N * M, 128),
            weights,
            tables,
        )

    first, values, cot, weights, tables, wide_map, wide_bias = vmem_call(
        analyse_kernel,
        "analyse",
        (
            SPECTRA,
            shape(grid_shape, BF),
            shape(grid_shape, BF),
            shape((M, K * C, 2 * C), BF),
            shape(PACKED.shape, BF),
            shape((2 * C, 2 * C), BF),
            shape((1, 2 * C)),
        ),
        [ROWS, pltpu.VMEM((C, C), BF), pltpu.VMEM((1, C), F32), pltpu.SemaphoreType.DMA((7,))],
        field.reshape(grid_shape),
        cotangent.reshape(grid_shape),
        mode_weights.reshape(M, K * C, 2 * C),
        jnp.asarray(PACKED),
        w_local,
        bias.reshape(1, C),
        specs=[IN_HBM] * 6,
    )
    u_hat, mixed = spectral(False, exchange(first))
    u_near, u_far = gather_samples(u_hat)
    gz, second = vmem_call(
        middle_kernel,
        "middle",
        (shape(grid_shape, BF), SPECTRA),
        [ROWS, ROWS],
        exchange(mixed.reshape(SPECTRA.shape)),
        values,
        cot,
        wide_map,
        wide_bias,
        tables,
    )
    g_hat, back = spectral(True, exchange(second))
    g_near, g_far = gather_samples(g_hat)
    grad_field = vmem_call(
        final_kernel,
        "final",
        shape(grid_shape, BF),
        [ROWS],
        exchange(back.reshape(SPECTRA.shape)),
        gz,
        wide_map,
        tables,
    )
    grad_modes = pl.pallas_call(
        grads_kernel,
        name="weight_grads",
        grid=(M // G_MODES,),
        out_shape=shape((M, K, C, 2 * C)),
        in_specs=[IN_VMEM] * 4,
        out_specs=pl.BlockSpec((G_MODES, K, C, 2 * C), lambda m: (m, 0, 0, 0)),
        compiler_params=PARAMS,
    )(u_near, u_far, g_near, g_far)
    return grad_field.reshape(field.shape), grad_modes


def solution(mesh):
    placed = (
        P("dp", "slab", None, None),
        P("dp", "slab", None, None),
        P("slab", None, None, None),
        P(),
        P(),
    )
    return jax.shard_map(
        body,
        mesh=mesh,
        in_specs=placed,
        out_specs=(P("dp", "slab", None, None), P("slab", None, None, None)),
        check_vma=False,
    )
```

```python
import math

import jax
import jax.numpy as jnp
import ml_dtypes
import numpy as np
from jax import lax
from jax.experimental import pallas as pl
from jax.experimental.pallas import tpu as pltpu
from jax.sharding import PartitionSpec as P

C = 64
K = 16
N = 64
CX = 2
SLABS = 32
DP = 8
TP = N // 2

BF = jnp.bfloat16
F32 = jnp.float32
SQRT_TWO_PI = math.sqrt(2.0 / math.pi)


def trig(freqs):
    phase = (freqs[:, None] * np.arange(N)[None, :] % N) * (2.0 * math.pi / N)
    return np.cos(phase) / math.sqrt(N), np.sin(phase) / math.sqrt(N)


def rounded(table):
    return table.astype(np.float32).astype(ml_dtypes.bfloat16)


def wide(table):
    high = rounded(table)
    low = rounded(table - high.astype(np.float64))
    return np.concatenate([high, low, high], 1)


def twice_table(table):
    high = rounded(table)
    low = rounded(table - high.astype(np.float64))
    return np.concatenate([high, low], 1)


SIGNED = np.concatenate([np.arange(K // 2), np.arange(-K // 2, 0)])
COS, SIN = trig(SIGNED)
T_COS, T_SIN = trig(np.arange(K))
P_RE, P_IM = T_COS.T, -T_SIN.T

Y_IN = twice_table(np.stack([COS, SIN], 1).reshape(2 * K, N))
Y_OUT = wide(np.concatenate([COS, SIN], 0).T)
X_IN = wide(np.concatenate([COS, SIN], 0))
X_OUT = wide(np.concatenate([COS, SIN], 0).T)


def t_in():
    re = rounded(P_RE).astype(np.float64).reshape(TP, 2, K)
    im = rounded(P_IM).astype(np.float64).reshape(TP, 2, K)
    rows_re = np.concatenate([re, im], 0)
    rows_im = np.concatenate([im, -re], 0)
    both = np.stack([rows_re, rows_im], 0)
    table = both.transpose(0, 2, 3, 1).reshape(4 * K, 2 * TP)
    return rounded(np.concatenate([table, table], 1))


def t_out():
    re = P_RE.reshape(TP, 2, K)
    im = P_IM.reshape(TP, 2, K)
    of_c = np.stack([re, im], 2)
    of_s = np.stack([im, -re], 2)
    return wide(np.concatenate([of_c, of_s], 0).reshape(2 * TP, 4 * K))


TABLES = {
    "y_in": Y_IN,
    "t_in": t_in(),
    "y_out": Y_OUT,
    "x_in": X_IN,
    "x_out": X_OUT,
    "t_out": t_out(),
}
PLACES = {}
for name, values in TABLES.items():
    PLACES[name] = (sum(TABLES[other].shape[0] for other in PLACES), *values.shape)
PACKED = np.concatenate([np.pad(v, ((0, 0), (0, 256 - v.shape[1]))) for v in TABLES.values()], 0)


def table(ref, name):
    first, rows, columns = PLACES[name]
    return ref[first : first + rows, :columns]


def dot(left, right):
    return jnp.dot(left, right, preferred_element_type=F32)


def split(data):
    high = data.astype(BF)
    return high, (data - high.astype(F32)).astype(BF)


def stack3(data):
    high, low = split(data)
    return jnp.concatenate([high, high, low], 0)


def stack2(data):
    high, low = split(data)
    return jnp.concatenate([high, low], 0)


def low_lanes(shape):
    return lax.broadcasted_iota(jnp.int32, shape, 1) < C


def swap(data):
    return pltpu.roll(data, C, 1)


def turned(data):
    other = swap(data)
    return jnp.where(low_lanes(data.shape), -other, other)


def lanes(blocks):
    return jnp.concatenate(blocks, 1)


Y_TILES = 8


def y_analysis_store(chunk, first_tile, tiles, y_in, scratch):
    out = dot(y_in, jnp.concatenate([chunk, chunk], 0))
    for j in range(tiles):
        scratch[pl.ds(first_tile + j, 2 * K, stride=TP), :] = out[:, j * 128 : (j + 1) * 128]


def t_analysis(scratch, t_table, out_ref, x, group=4):
    low = low_lanes((K, 128))
    for first in range(0, K, group):
        data = lanes([scratch[(first + j) * 2 * TP : (first + j + 1) * 2 * TP, :] for j in range(group)])
        res = dot(t_table, stack2(data))
        for j in range(group):
            re0, re1, im0, im1 = (res[q * K : (q + 1) * K, j * 128 : (j + 1) * 128] for q in range(4))
            both = jnp.where(low, re0, im1) + swap(jnp.where(low, im0, re1))
            out_ref[2 * (first + j), x] = both[:8]
            out_ref[2 * (first + j) + 1, x] = both[8:]


def t_synthesis(w_ref, t_table, scratch, x, group=4):
    low = low_lanes((K, 128))
    zero = jnp.zeros((K, 128), F32)
    for first in range(0, K, group):
        blocks = []
        for j in range(group):
            w = jnp.concatenate([w_ref[2 * (first + j), x], w_ref[2 * (first + j) + 1, x]], 0)
            other = swap(w)
            blocks.append(
                jnp.concatenate(
                    [
                        jnp.where(low, w, zero),
                        jnp.where(low, other, zero),
                        jnp.where(low, zero, other),
                        jnp.where(low, zero, w),
                    ],
                    0,
                )
            )
        res = dot(t_table, stack3(lanes(blocks)))
        for j in range(group):
            for cs in range(2):
                scratch[pl.ds(cs * K + first + j, TP, stride=2 * K), :] = res[
                    cs * TP : (cs + 1) * TP, j * 128 : (j + 1) * 128
                ]


def y_synthesis(scratch, first_tile, tiles, y_out):
    data = lanes(
        [
            scratch[pl.ds(pl.multiple_of((first_tile + j) * 2 * K, 2 * K), 2 * K), :]
            for j in range(tiles)
        ]
    )
    return dot(y_out, stack3(data))


def channel_map(chunk, weight, tiles, contracted=0):
    rows = jnp.concatenate([chunk[:, j * 128 : (j + 1) * 128] for j in range(tiles)], 0)
    out = lax.dot_general(
        rows, weight, (((1,), (contracted,)), ((), ())), preferred_element_type=F32
    )
    return lanes([out[j * N : (j + 1) * N] for j in range(tiles)])


def lane_slice(step, tiles):
    return pl.ds(pl.multiple_of(step * tiles * 128, tiles * 128), tiles * 128)


HALF = N * C // 2


def start_all(sems, *moves):
    copies = [pltpu.make_async_copy(*move, sems.at[i]) for i, move in enumerate(moves)]
    for copy in copies:
        copy.start()
    return copies


def analyse_kernel(
    field_in, w_in, tables_in, map_in, bias_in,
    out_ref, w_ref, tables_ref, map_ref, bias_ref,
    field, scratch, small_map, small_bias, sems,
):
    parts = [(i // 2, slice(None), pl.ds(i % 2 * HALF, HALF)) for i in range(2 * CX)]
    copies = start_all(
        sems,
        (tables_in, tables_ref),
        *((field_in.at[part], field.at[part]) for part in parts),
        (map_in, small_map),
        (bias_in, small_bias),
        (w_in, w_ref),
    )
    copies[0].wait()
    y_in, t_in = table(tables_ref, "y_in"), table(tables_ref, "t_in")
    for i in range(2 * CX):
        copies[1 + i].wait()

        @pl.loop(i % 2 * TP // 2 // Y_TILES, (i % 2 + 1) * TP // 2 // Y_TILES)
        def _(step):
            y_analysis_store(
                field[i // 2, :, lane_slice(step, Y_TILES)], step * Y_TILES, Y_TILES, y_in, scratch
            )

        if i % 2 == 1:
            t_analysis(scratch, t_in, out_ref, i // 2)
    for copy in copies[1 + 2 * CX :]:
        copy.wait()
    wide_map = jnp.concatenate([small_map[...]] * 2, 1)
    wide_map = jnp.concatenate([wide_map] * 2, 0)
    row = lax.broadcasted_iota(jnp.int32, (2 * C, 2 * C), 0) // C
    lane = lax.broadcasted_iota(jnp.int32, (2 * C, 2 * C), 1) // C
    map_ref[...] = jnp.where(row == lane, wide_map, jnp.zeros_like(wide_map))
    bias_ref[...] = jnp.concatenate([small_bias[...]] * 2, 1)


def gelu_slope(z):
    square = z * z
    tanh_value = jnp.tanh(z * (SQRT_TWO_PI + SQRT_TWO_PI * 0.044715 * square))
    inner_slope = z * (0.5 * SQRT_TWO_PI + 1.5 * SQRT_TWO_PI * 0.044715 * square)
    return 0.5 + 0.5 * tanh_value + inner_slope * (1.0 - tanh_value * tanh_value)


def middle_kernel(
    w_ref, field_in, cot_in, map_ref, bias_ref, tables_ref, gz_out, out_ref, field, cot, gz, syn, ana, sems
):
    copies = start_all(
        sems,
        (field_in.at[0], field.at[0]),
        (cot_in.at[0], cot.at[0]),
        (field_in.at[1], field.at[1]),
        (cot_in.at[1], cot.at[1]),
    )
    backs = [pltpu.make_async_copy(gz.at[x], gz_out.at[x], sems.at[len(copies) + x]) for x in range(CX)]
    y_in, y_out, t_in, t_out = (table(tables_ref, name) for name in ("y_in", "y_out", "t_in", "t_out"))
    for x in range(CX):
        t_synthesis(w_ref, t_out, syn, x)
        copies[2 * x].wait()
        copies[2 * x + 1].wait()

        @pl.loop(0, TP // Y_TILES)
        def _(step):
            at = lane_slice(step, Y_TILES)
            spec = y_synthesis(syn, step * Y_TILES, Y_TILES, y_out)
            z = spec + channel_map(field[x, :, at], map_ref[...], Y_TILES) + lanes([bias_ref[...]] * Y_TILES)
            out = (cot[x, :, at].astype(F32) * gelu_slope(z)).astype(BF)
            gz[x, :, at] = out
            y_analysis_store(out, step * Y_TILES, Y_TILES, y_in, ana)

        backs[x].start()
        t_analysis(ana, t_in, out_ref, x)
    for back in backs:
        back.wait()


def final_kernel(w_ref, gz_in, map_ref, tables_ref, grad_out, gz, grad, syn, sems):
    copies = start_all(sems, (gz_in.at[0], gz.at[0]), (gz_in.at[1], gz.at[1]))
    backs = [
        pltpu.make_async_copy(grad.at[x], grad_out.at[x], sems.at[len(copies) + x]) for x in range(CX)
    ]
    y_out, t_out = table(tables_ref, "y_out"), table(tables_ref, "t_out")
    for x in range(CX):
        t_synthesis(w_ref, t_out, syn, x)
        copies[x].wait()

        @pl.loop(0, TP // Y_TILES)
        def _(step):
            at = lane_slice(step, Y_TILES)
            spec = y_synthesis(syn, step * Y_TILES, Y_TILES, y_out)
            grad[x, :, at] = (spec + channel_map(gz[x, :, at], map_ref[...], Y_TILES, 1)).astype(BF)

        backs[x].start()
    for back in backs:
        back.wait()


M = 8


def x_analysis(in_ref, x_in):
    data = lanes([in_ref[pl.ds(m, N, stride=M), :] for m in range(M)])
    res = dot(x_in, stack3(data))
    out = []
    for m in range(M):
        cos_part = res[:K, m * 128 : (m + 1) * 128]
        sin_part = res[K:, m * 128 : (m + 1) * 128]
        out.append(cos_part - turned(sin_part))
    return out


def x_synthesis(blocks, x_out, out_ref):
    data = lanes([jnp.concatenate([v, turned(v)], 0) for v in blocks])
    res = dot(x_out, stack3(data))
    for m in range(M):
        out_ref[pl.ds(m, N, stride=M), :] = res[:, m * 128 : (m + 1) * 128]


def mix(u, weights):
    low = low_lanes((K, 128))
    other = swap(u)
    rows = jnp.concatenate([jnp.where(low, u, other), jnp.where(low, other, u)], 0)
    parts = jnp.concatenate(split(rows), 0).astype(F32)
    row = lax.broadcasted_iota(jnp.int32, (4 * K, 128), 0) % K
    half = lax.broadcasted_iota(jnp.int32, (4 * K, 128), 1) // C
    left = lanes([jnp.where(row == 2 * j + half, parts, 0.0).astype(BF) for j in range(K // 2)])
    res = dot(left, weights)
    res = res[: 2 * K] + res[2 * K :]
    return res[:K] + turned(res[K:])


def mix_adjoint(g, weights):
    rows = jnp.concatenate([g, -turned(g)], 0)
    parts = jnp.concatenate(split(rows), 0)
    res = lax.dot_general(parts, weights, (((1,), (1,)), ((), ())), preferred_element_type=F32)
    res = res[: 2 * K] + res[2 * K :]
    row = lax.broadcasted_iota(jnp.int32, (2 * K, 128), 0) % K
    half = lax.broadcasted_iota(jnp.int32, (2 * K, 128), 1) // C
    total = jnp.zeros((2 * K, 128), F32)
    for j in range(K // 2):
        total = total + jnp.where(row == 2 * j + half, res[:, j * 128 : (j + 1) * 128], 0.0)
    total = total + swap(total)
    return jnp.where(low_lanes((K, 128)), total[:K], total[K:])


def spectral_kernel(adjoint, in_ref, w_ref, tables_ref, hat_ref, out_ref):
    spectra = x_analysis(in_ref, table(tables_ref, "x_in"))
    mixed = []
    for m in range(M):
        hat_ref[m] = spectra[m]
        weights = w_ref[m]
        mixed.append(mix_adjoint(spectra[m], weights) if adjoint else mix(spectra[m], weights))
    x_synthesis(mixed, table(tables_ref, "x_out"), out_ref)


G_MODES = 2


def grads_kernel(*refs):
    u_refs, g_refs, out_ref = refs[:Y_RING], refs[Y_RING : 2 * Y_RING], refs[-1]
    own = lax.broadcasted_iota(jnp.int32, (C, 2 * DP * K), 1) % K // 2
    odd = lax.broadcasted_iota(jnp.int32, (2 * DP * K, 1), 0) % 2 == 1
    for j in range(G_MODES):
        m = pl.program_id(0) * G_MODES + j
        u, g = (
            jnp.concatenate([ref[b, m] for ref in part for b in range(DP // Y_RING)], 0)
            for part in (u_refs, g_refs)
        )
        u_t = u.T.astype(BF)
        left = lanes([u_t[:C], u_t[C:]])
        right = jnp.concatenate([g, -turned(g)], 0)
        right = lanes([jnp.where(odd, 0.0, right), jnp.where(odd, right, 0.0)]).astype(BF)
        tall = jnp.concatenate([jnp.where(own == q, left, jnp.zeros_like(left)) for q in range(K // 2)], 0)
        out = dot(tall, right)
        for kx in range(K):
            out_ref[j, kx] = out[kx // 2 * C : (kx // 2 + 1) * C, kx % 2 * 128 : (kx % 2 + 1) * 128]


LIMIT = 32
IN_VMEM = pl.BlockSpec(memory_space=pltpu.VMEM)
IN_HBM = pl.BlockSpec(memory_space=pltpu.HBM)


def call(kernel, name, out_shapes, out_specs, scratch, *operands, specs):
    return pl.pallas_call(
        kernel,
        name=name,
        out_shape=out_shapes,
        in_specs=specs,
        out_specs=out_specs,
        scratch_shapes=scratch,
        compiler_params=pltpu.CompilerParams(vmem_limit_bytes=LIMIT * 2**20),
    )(*operands)


def in_vmem(*arrays):
    return [pltpu.with_memory_space_constraint(array, pltpu.VMEM) for array in arrays]


def in_hbm(*arrays):
    return [pltpu.with_memory_space_constraint(array, pltpu.HBM) for array in arrays]


def shape(dims, kind=F32):
    return jax.ShapeDtypeStruct(dims, kind)


SPECTRA = shape((SLABS, CX, M, 128))
ROWS = pltpu.VMEM((TP * 2 * K, 128), F32)
Y_RING = 4


def exchange(data):
    return lax.all_to_all(data, "slab", 0, 0, tiled=True)


def x_pair(data):
    return jnp.stack([data, lax.ppermute(data, "dp", [(i, (i + Y_RING) % DP) for i in range(DP)])], 0)


def y_ring(data):
    def moved(by):
        return lax.ppermute(
            data, "dp", [(i, i // Y_RING * Y_RING + (i + by) % Y_RING) for i in range(DP)]
        )

    return [data, moved(1), moved(3), moved(2)]


def body(field, cotangent, mode_weights, w_local, bias):
    grid_shape = (CX, N, N * C)
    on_grid = pltpu.VMEM(grid_shape, BF)
    values, cot = field.reshape(grid_shape), cotangent.reshape(grid_shape)

    def spectral(adjoint, data):
        return call(
            lambda *refs: spectral_kernel(adjoint, *refs),
            "adjoint" if adjoint else "mix",
            (shape((M, K, 128)), shape((N * M, 128))),
            [IN_VMEM] * 2,
            [],
            data.reshape(N * M, 128),
            *in_vmem(weights, tables),
            specs=[IN_VMEM] * 3,
        )

    first, weights, tables, wide_map, wide_bias = call(
        analyse_kernel,
        "analyse",
        (
            SPECTRA,
            pltpu.VMEM((M, K * C, 2 * C), BF),
            pltpu.VMEM(PACKED.shape, BF),
            pltpu.VMEM((2 * C, 2 * C), BF),
            pltpu.VMEM((1, 2 * C), F32),
        ),
        [IN_VMEM] * 5,
        [on_grid, ROWS, pltpu.VMEM((C, C), BF), pltpu.VMEM((1, C), F32), pltpu.SemaphoreType.DMA((8,))],
        *in_hbm(
            values, mode_weights.reshape(M, K * C, 2 * C), jnp.asarray(PACKED), w_local, bias.reshape(1, C)
        ),
        specs=[IN_HBM] * 5,
    )
    u_hat, mixed = spectral(False, exchange(first))
    u_pair = x_pair(u_hat)
    arrived, u_pair = lax.optimization_barrier((exchange(mixed.reshape(SPECTRA.shape)), u_pair))
    gz, second = call(
        middle_kernel,
        "middle",
        (pltpu.HBM(grid_shape, BF), SPECTRA),
        [IN_HBM, IN_VMEM],
        [on_grid, on_grid, on_grid, ROWS, ROWS, pltpu.SemaphoreType.DMA((6,))],
        arrived,
        *in_hbm(values, cot),
        *in_vmem(wide_map, wide_bias, tables),
        specs=[IN_VMEM] + [IN_HBM] * 2 + [IN_VMEM] * 3,
    )
    u_all = y_ring(u_pair)
    arrived, u_all = lax.optimization_barrier((exchange(second), u_all))
    g_hat, back = spectral(True, arrived)
    g_all = y_ring(x_pair(g_hat))
    grad_field = call(
        final_kernel,
        "final",
        pltpu.HBM(grid_shape, BF),
        IN_HBM,
        [on_grid, on_grid, ROWS, pltpu.SemaphoreType.DMA((4,))],
        exchange(back.reshape(SPECTRA.shape)),
        *in_hbm(gz),
        *in_vmem(wide_map, tables),
        specs=[IN_VMEM, IN_HBM] + [IN_VMEM] * 2,
    )
    grad_field, g_all = lax.optimization_barrier((grad_field, g_all))
    grad_modes = pl.pallas_call(
        grads_kernel,
        name="weight_grads",
        grid=(M // G_MODES,),
        out_shape=shape((M, K, C, 2 * C)),
        in_specs=[IN_VMEM] * 2 * Y_RING,
        out_specs=pl.BlockSpec((G_MODES, K, C, 2 * C), lambda m: (m, 0, 0, 0)),
        compiler_params=pltpu.CompilerParams(vmem_limit_bytes=LIMIT * 2**20),
    )(*u_all, *g_all)
    return grad_field.reshape(field.shape), grad_modes


def solution(mesh):
    placed = (
        P("dp", "slab", None, None),
        P("dp", "slab", None, None),
        P("slab", None, None, None),
        P(),
        P(),
    )
    return jax.shard_map(
        body,
        mesh=mesh,
        in_specs=placed,
        out_specs=(P("dp", "slab", None, None), P("slab", None, None, None)),
        check_vma=False,
    )
```

```python
import math

import jax
import jax.numpy as jnp
import ml_dtypes
import numpy as np
from jax import lax
from jax.experimental import pallas as pl
from jax.experimental.pallas import tpu as pltpu
from jax.sharding import PartitionSpec as P

C = 64
K = 16
N = 64
CX = 2
SLABS = 32
DP = 8
TP = N // 2

BF = jnp.bfloat16
F32 = jnp.float32
SQRT_TWO_PI = math.sqrt(2.0 / math.pi)


def trig(freqs):
    phase = (freqs[:, None] * np.arange(N)[None, :] % N) * (2.0 * math.pi / N)
    return np.cos(phase) / math.sqrt(N), np.sin(phase) / math.sqrt(N)


def rounded(table):
    return table.astype(np.float32).astype(ml_dtypes.bfloat16)


def wide(table):
    high = rounded(table)
    low = rounded(table - high.astype(np.float64))
    return np.concatenate([high, low, high], 1)


def twice_table(table):
    high = rounded(table)
    low = rounded(table - high.astype(np.float64))
    return np.concatenate([high, low], 1)


SIGNED = np.concatenate([np.arange(K // 2), np.arange(-K // 2, 0)])
COS, SIN = trig(SIGNED)
T_COS, T_SIN = trig(np.arange(K))
P_RE, P_IM = T_COS.T, -T_SIN.T

Y_IN = twice_table(np.stack([COS, SIN], 1).reshape(2 * K, N))
Y_OUT = wide(np.concatenate([COS, SIN], 0).T)
X_IN = wide(np.concatenate([COS, SIN], 0))
X_OUT = wide(np.concatenate([COS, SIN], 0).T)


def t_in():
    re = rounded(P_RE).astype(np.float64).reshape(TP, 2, K)
    im = rounded(P_IM).astype(np.float64).reshape(TP, 2, K)
    rows_re = np.concatenate([re, im], 0)
    rows_im = np.concatenate([im, -re], 0)
    both = np.stack([rows_re, rows_im], 0)
    table = both.transpose(0, 2, 3, 1).reshape(4 * K, 2 * TP)
    return rounded(np.concatenate([table, table], 1))


def t_out():
    re = P_RE.reshape(TP, 2, K)
    im = P_IM.reshape(TP, 2, K)
    of_c = np.stack([re, im], 2)
    of_s = np.stack([im, -re], 2)
    return wide(np.concatenate([of_c, of_s], 0).reshape(2 * TP, 4 * K))


TABLES = {
    "y_in": Y_IN,
    "t_in": t_in(),
    "y_out": Y_OUT,
    "x_in": X_IN,
    "x_out": X_OUT,
    "t_out": t_out(),
}
PLACES = {}
for name, values in TABLES.items():
    PLACES[name] = (sum(TABLES[other].shape[0] for other in PLACES), *values.shape)
PACKED = np.concatenate([np.pad(v, ((0, 0), (0, 256 - v.shape[1]))) for v in TABLES.values()], 0)


def table(ref, name):
    first, rows, columns = PLACES[name]
    return ref[first : first + rows, :columns]


def dot(left, right):
    return jnp.dot(left, right, preferred_element_type=F32)


def split(data):
    high = data.astype(BF)
    return high, (data - high.astype(F32)).astype(BF)


def stack3(data):
    high, low = split(data)
    return jnp.concatenate([high, high, low], 0)


def stack2(data):
    high, low = split(data)
    return jnp.concatenate([high, low], 0)


def low_lanes(shape):
    return lax.broadcasted_iota(jnp.int32, shape, 1) < C


def swap(data):
    return pltpu.roll(data, C, 1)


def turned(data):
    other = swap(data)
    return jnp.where(low_lanes(data.shape), -other, other)


def lanes(blocks):
    return jnp.concatenate(blocks, 1)


def steps(first, last):
    def run(step_of):
        for step in range(first, last):
            step_of(step)

    return run


Y_TILES = 16


def y_analysis_store(chunk, first_tile, tiles, y_in, scratch):
    out = dot(y_in, jnp.concatenate([chunk, chunk], 0))
    for j in range(tiles):
        scratch[pl.ds(first_tile + j, 2 * K, stride=TP), :] = out[:, j * 128 : (j + 1) * 128]


def t_analysis(scratch, t_table, out_ref, x, group=16):
    low = low_lanes((K, 128))
    for first in range(0, K, group):
        data = lanes([scratch[(first + j) * 2 * TP : (first + j + 1) * 2 * TP, :] for j in range(group)])
        res = dot(t_table, stack2(data))
        for j in range(group):
            re0, re1, im0, im1 = (res[q * K : (q + 1) * K, j * 128 : (j + 1) * 128] for q in range(4))
            both = jnp.where(low, re0, im1) + swap(jnp.where(low, im0, re1))
            out_ref[2 * (first + j), x] = both[:8]
            out_ref[2 * (first + j) + 1, x] = both[8:]


def t_synthesis(w_ref, t_table, scratch, x, group=16):
    low = low_lanes((K, 128))
    zero = jnp.zeros((K, 128), F32)
    for first in range(0, K, group):
        blocks = []
        for j in range(group):
            w = jnp.concatenate([w_ref[2 * (first + j), x], w_ref[2 * (first + j) + 1, x]], 0)
            other = swap(w)
            blocks.append(
                jnp.concatenate(
                    [
                        jnp.where(low, w, zero),
                        jnp.where(low, other, zero),
                        jnp.where(low, zero, other),
                        jnp.where(low, zero, w),
                    ],
                    0,
                )
            )
        res = dot(t_table, stack3(lanes(blocks)))
        for j in range(group):
            for cs in range(2):
                scratch[pl.ds(cs * K + first + j, TP, stride=2 * K), :] = res[
                    cs * TP : (cs + 1) * TP, j * 128 : (j + 1) * 128
                ]


def y_synthesis(scratch, first_tile, tiles, y_out):
    data = lanes(
        [
            scratch[pl.ds((first_tile + j) * 2 * K, 2 * K), :]
            for j in range(tiles)
        ]
    )
    return dot(y_out, stack3(data))


def channel_map(chunk, weight, tiles, contracted=0):
    rows = jnp.concatenate([chunk[:, j * 128 : (j + 1) * 128] for j in range(tiles)], 0)
    out = lax.dot_general(
        rows, weight, (((1,), (contracted,)), ((), ())), preferred_element_type=F32
    )
    return lanes([out[j * N : (j + 1) * N] for j in range(tiles)])


def lane_slice(step, tiles):
    return pl.ds(step * tiles * 128, tiles * 128)


HALF = N * C // 2


def start_all(sems, *moves):
    copies = [pltpu.make_async_copy(*move, sems.at[i]) for i, move in enumerate(moves)]
    for copy in copies:
        copy.start()
    return copies


def analyse_kernel(
    field_in, w_in, tables_in, map_in, bias_in,
    out_ref, w_ref, tables_ref, map_ref, bias_ref,
    field, scratch, small_map, small_bias, sems,
):
    parts = [(i // 2, slice(None), pl.ds(i % 2 * HALF, HALF)) for i in range(2 * CX)]
    copies = start_all(
        sems,
        (tables_in, tables_ref),
        *((field_in.at[part], field.at[part]) for part in parts),
        (map_in, small_map),
        (bias_in, small_bias),
        (w_in, w_ref),
    )
    copies[0].wait()
    y_in, t_in = table(tables_ref, "y_in"), table(tables_ref, "t_in")
    for i in range(2 * CX):
        copies[1 + i].wait()

        @steps(i % 2 * TP // 2 // Y_TILES, (i % 2 + 1) * TP // 2 // Y_TILES)
        def _(step):
            y_analysis_store(
                field[i // 2, :, lane_slice(step, Y_TILES)], step * Y_TILES, Y_TILES, y_in, scratch
            )

        if i % 2 == 1:
            t_analysis(scratch, t_in, out_ref, i // 2)
    for copy in copies[1 + 2 * CX :]:
        copy.wait()
    wide_map = jnp.concatenate([small_map[...]] * 2, 1)
    wide_map = jnp.concatenate([wide_map] * 2, 0)
    row = lax.broadcasted_iota(jnp.int32, (2 * C, 2 * C), 0) // C
    lane = lax.broadcasted_iota(jnp.int32, (2 * C, 2 * C), 1) // C
    map_ref[...] = jnp.where(row == lane, wide_map, jnp.zeros_like(wide_map))
    bias_ref[...] = jnp.concatenate([small_bias[...]] * 2, 1)


def gelu_slope(z):
    square = z * z
    tanh_value = jnp.tanh(z * (SQRT_TWO_PI + SQRT_TWO_PI * 0.044715 * square))
    inner_slope = z * (0.5 * SQRT_TWO_PI + 1.5 * SQRT_TWO_PI * 0.044715 * square)
    return 0.5 + 0.5 * tanh_value + inner_slope * (1.0 - tanh_value * tanh_value)


def middle_kernel(
    w_ref, field_in, cot_in, map_ref, bias_ref, tables_ref, gz_out, out_ref, field, cot, gz, syn, ana, sems
):
    copies = start_all(
        sems,
        (field_in.at[0], field.at[0]),
        (cot_in.at[0], cot.at[0]),
        (field_in.at[1], field.at[1]),
        (cot_in.at[1], cot.at[1]),
    )
    backs = [pltpu.make_async_copy(gz.at[x], gz_out.at[x], sems.at[len(copies) + x]) for x in range(CX)]
    y_in, y_out, t_in, t_out = (table(tables_ref, name) for name in ("y_in", "y_out", "t_in", "t_out"))
    for x in range(CX):
        t_synthesis(w_ref, t_out, syn, x)
        copies[2 * x].wait()
        copies[2 * x + 1].wait()

        @steps(0, TP // Y_TILES)
        def _(step):
            at = lane_slice(step, Y_TILES)
            spec = y_synthesis(syn, step * Y_TILES, Y_TILES, y_out)
            z = spec + channel_map(field[x, :, at], map_ref[...], Y_TILES) + lanes([bias_ref[...]] * Y_TILES)
            out = (cot[x, :, at].astype(F32) * gelu_slope(z)).astype(BF)
            gz[x, :, at] = out
            y_analysis_store(out, step * Y_TILES, Y_TILES, y_in, ana)

        backs[x].start()
        t_analysis(ana, t_in, out_ref, x)
    for back in backs:
        back.wait()


def final_kernel(w_ref, gz_in, map_ref, tables_ref, grad_out, gz, grad, syn, sems):
    copies = start_all(sems, (gz_in.at[0], gz.at[0]), (gz_in.at[1], gz.at[1]))
    backs = [
        pltpu.make_async_copy(grad.at[x], grad_out.at[x], sems.at[len(copies) + x]) for x in range(CX)
    ]
    y_out, t_out = table(tables_ref, "y_out"), table(tables_ref, "t_out")
    for x in range(CX):
        t_synthesis(w_ref, t_out, syn, x)
        copies[x].wait()

        @steps(0, TP // Y_TILES)
        def _(step):
            at = lane_slice(step, Y_TILES)
            spec = y_synthesis(syn, step * Y_TILES, Y_TILES, y_out)
            grad[x, :, at] = (spec + channel_map(gz[x, :, at], map_ref[...], Y_TILES, 1)).astype(BF)

        backs[x].start()
    for back in backs:
        back.wait()


M = 8


def x_analysis(in_ref, x_in):
    data = lanes([in_ref[pl.ds(m, N, stride=M), :] for m in range(M)])
    res = dot(x_in, stack3(data))
    out = []
    for m in range(M):
        cos_part = res[:K, m * 128 : (m + 1) * 128]
        sin_part = res[K:, m * 128 : (m + 1) * 128]
        out.append(cos_part - turned(sin_part))
    return out


def x_synthesis(blocks, x_out, out_ref):
    data = lanes([jnp.concatenate([v, turned(v)], 0) for v in blocks])
    res = dot(x_out, stack3(data))
    for m in range(M):
        out_ref[pl.ds(m, N, stride=M), :] = res[:, m * 128 : (m + 1) * 128]


def mix(u, weights):
    low = low_lanes((K, 128))
    other = swap(u)
    rows = jnp.concatenate([jnp.where(low, u, other), jnp.where(low, other, u)], 0)
    parts = jnp.concatenate(split(rows), 0).astype(F32)
    row = lax.broadcasted_iota(jnp.int32, (4 * K, 128), 0) % K
    half = lax.broadcasted_iota(jnp.int32, (4 * K, 128), 1) // C
    left = lanes([jnp.where(row == 2 * j + half, parts, 0.0).astype(BF) for j in range(K // 2)])
    res = dot(left, weights)
    res = res[: 2 * K] + res[2 * K :]
    return res[:K] + turned(res[K:])


def mix_adjoint(g, weights):
    rows = jnp.concatenate([g, -turned(g)], 0)
    parts = jnp.concatenate(split(rows), 0)
    res = lax.dot_general(parts, weights, (((1,), (1,)), ((), ())), preferred_element_type=F32)
    res = res[: 2 * K] + res[2 * K :]
    row = lax.broadcasted_iota(jnp.int32, (2 * K, 128), 0) % K
    half = lax.broadcasted_iota(jnp.int32, (2 * K, 128), 1) // C
    total = jnp.zeros((2 * K, 128), F32)
    for j in range(K // 2):
        total = total + jnp.where(row == 2 * j + half, res[:, j * 128 : (j + 1) * 128], 0.0)
    total = total + swap(total)
    return jnp.where(low_lanes((K, 128)), total[:K], total[K:])


def mix_kernel(in_ref, w_ref, tables_ref, hat_ref, out_ref):
    spectra = x_analysis(in_ref, table(tables_ref, "x_in"))
    mixed = []
    for m in range(M):
        hat_ref[m] = spectra[m]
        mixed.append(mix(spectra[m], w_ref[m]))
    x_synthesis(mixed, table(tables_ref, "x_out"), out_ref)


def adjoint_kernel(in_ref, u_ref, w_ref, tables_ref, hats_ref, out_ref):
    spectra = x_analysis(in_ref, table(tables_ref, "x_in"))
    mixed = []
    for m in range(M):
        hats_ref[0, m] = u_ref[m]
        hats_ref[1, m] = spectra[m]
        mixed.append(mix_adjoint(spectra[m], w_ref[m]))
    x_synthesis(mixed, table(tables_ref, "x_out"), out_ref)


def grads_kernel(*refs):
    hats, (grads_out, grads, sems) = refs[:DP], refs[DP:]
    own = lax.broadcasted_iota(jnp.int32, (C, 2 * DP * K), 1) % K // 2
    odd = lax.broadcasted_iota(jnp.int32, (2 * DP * K, 1), 0) % 2 == 1
    copies = [pltpu.make_async_copy(grads.at[m], grads_out.at[m], sems.at[m]) for m in range(M)]
    for m in range(M):
        u, g = (jnp.concatenate([hat[i, m] for hat in hats], 0) for i in range(2))
        u_t = u.T.astype(BF)
        left = lanes([u_t[:C], u_t[C:]])
        right = jnp.concatenate([g, -turned(g)], 0)
        right = lanes([jnp.where(odd, 0.0, right), jnp.where(odd, right, 0.0)]).astype(BF)
        tall = jnp.concatenate([jnp.where(own == q, left, jnp.zeros_like(left)) for q in range(K // 2)], 0)
        out = dot(tall, right)
        for kx in range(K):
            grads[m, kx] = out[kx // 2 * C : (kx // 2 + 1) * C, kx % 2 * 128 : (kx % 2 + 1) * 128]
        copies[m].start()
    for copy in copies:
        copy.wait()


LIMIT = 32
IN_VMEM = pl.BlockSpec(memory_space=pltpu.VMEM)
IN_HBM = pl.BlockSpec(memory_space=pltpu.HBM)


def call(kernel, name, out_shapes, out_specs, scratch, *operands, specs):
    return pl.pallas_call(
        kernel,
        name=name,
        out_shape=out_shapes,
        in_specs=specs,
        out_specs=out_specs,
        scratch_shapes=scratch,
        compiler_params=pltpu.CompilerParams(vmem_limit_bytes=LIMIT * 2**20),
    )(*operands)


def in_vmem(*arrays):
    return [pltpu.with_memory_space_constraint(array, pltpu.VMEM) for array in arrays]


def in_hbm(*arrays):
    return [pltpu.with_memory_space_constraint(array, pltpu.HBM) for array in arrays]


def shape(dims, kind=F32):
    return jax.ShapeDtypeStruct(dims, kind)


SPECTRA = shape((SLABS, CX, M, 128))
ROWS = pltpu.VMEM((TP * 2 * K, 128), F32)


def exchange(data):
    return lax.all_to_all(data, "slab", 0, 0, tiled=True)


Y_RING = 4


def x_partner(data):
    return lax.ppermute(data, "dp", [(i, (i + Y_RING) % DP) for i in range(DP)])


def y_neighbours(data):
    return [
        lax.ppermute(data, "dp", [(i, i // Y_RING * Y_RING + (i + by) % Y_RING) for i in range(DP)])
        for by in (1, 3, 2)
    ]


def body(field, cotangent, mode_weights, w_local, bias):
    grid_shape = (CX, N, N * C)
    on_grid = pltpu.VMEM(grid_shape, BF)
    values, cot = field.reshape(grid_shape), cotangent.reshape(grid_shape)

    first, weights, tables, wide_map, wide_bias = call(
        analyse_kernel,
        "analyse",
        (
            SPECTRA,
            pltpu.VMEM((M, K * C, 2 * C), BF),
            pltpu.VMEM(PACKED.shape, BF),
            pltpu.VMEM((2 * C, 2 * C), BF),
            pltpu.VMEM((1, 2 * C), F32),
        ),
        [IN_VMEM] * 5,
        [on_grid, ROWS, pltpu.VMEM((C, C), BF), pltpu.VMEM((1, C), F32), pltpu.SemaphoreType.DMA((8,))],
        *in_hbm(
            values, mode_weights.reshape(M, K * C, 2 * C), jnp.asarray(PACKED), w_local, bias.reshape(1, C)
        ),
        specs=[IN_HBM] * 5,
    )
    u_hat, mixed = call(
        mix_kernel,
        "mix",
        (shape((M, K, 128)), shape((N * M, 128))),
        [IN_VMEM] * 2,
        [],
        exchange(first).reshape(N * M, 128),
        *in_vmem(weights, tables),
        specs=[IN_VMEM] * 3,
    )
    arrived = exchange(mixed.reshape(SPECTRA.shape))
    gz, second = call(
        middle_kernel,
        "middle",
        (pltpu.HBM(grid_shape, BF), SPECTRA),
        [IN_HBM, IN_VMEM],
        [on_grid, on_grid, on_grid, ROWS, ROWS, pltpu.SemaphoreType.DMA((6,))],
        arrived,
        *in_hbm(values, cot),
        *in_vmem(wide_map, wide_bias, tables),
        specs=[IN_VMEM] + [IN_HBM] * 2 + [IN_VMEM] * 3,
    )
    hats, back = call(
        adjoint_kernel,
        "adjoint",
        (shape((2, M, K, 128)), shape((N * M, 128))),
        [IN_VMEM] * 2,
        [],
        exchange(second).reshape(N * M, 128),
        u_hat,
        *in_vmem(weights, tables),
        specs=[IN_VMEM] * 4,
    )
    partner = x_partner(hats)
    others = [*y_neighbours(hats), partner, *y_neighbours(partner)]
    grad_field = call(
        final_kernel,
        "final",
        pltpu.HBM(grid_shape, BF),
        IN_HBM,
        [on_grid, on_grid, ROWS, pltpu.SemaphoreType.DMA((4,))],
        exchange(back.reshape(SPECTRA.shape)),
        *in_hbm(gz),
        *in_vmem(wide_map, tables),
        specs=[IN_VMEM, IN_HBM] + [IN_VMEM] * 2,
    )
    grad_field, *others = lax.optimization_barrier((grad_field, *others))
    grad_modes = call(
        grads_kernel,
        "weight_grads",
        pltpu.HBM((M, K, C, 2 * C), F32),
        IN_HBM,
        [pltpu.VMEM((M, K, C, 2 * C), F32), pltpu.SemaphoreType.DMA((M,))],
        hats,
        *others,
        specs=[IN_VMEM] * DP,
    )
    return grad_field.reshape(field.shape), grad_modes


def solution(mesh):
    placed = (
        P("dp", "slab", None, None),
        P("dp", "slab", None, None),
        P("slab", None, None, None),
        P(),
        P(),
    )
    return jax.shard_map(
        body,
        mesh=mesh,
        in_specs=placed,
        out_specs=(P("dp", "slab", None, None), P("slab", None, None, None)),
        check_vma=False,
    )
```

```python
import math

import jax
import jax.numpy as jnp
import ml_dtypes
import numpy as np
from jax import lax
from jax.experimental import pallas as pl
from jax.experimental.pallas import tpu as pltpu
from jax.sharding import PartitionSpec as P

C = 64
K = 16
N = 64
CX = 2
SLABS = 32
DP = 8
TP = N // 2

BF = jnp.bfloat16
F32 = jnp.float32
SQRT_TWO_PI = math.sqrt(2.0 / math.pi)


def trig(freqs):
    phase = (freqs[:, None] * np.arange(N)[None, :] % N) * (2.0 * math.pi / N)
    return np.cos(phase) / math.sqrt(N), np.sin(phase) / math.sqrt(N)


def rounded(table):
    return table.astype(np.float32).astype(ml_dtypes.bfloat16)


def wide(table):
    high = rounded(table)
    low = rounded(table - high.astype(np.float64))
    return np.concatenate([high, low, high], 1)


def twice_table(table):
    high = rounded(table)
    low = rounded(table - high.astype(np.float64))
    return np.concatenate([high, low], 1)


SIGNED = np.concatenate([np.arange(K // 2), np.arange(-K // 2, 0)])
COS, SIN = trig(SIGNED)
T_COS, T_SIN = trig(np.arange(K))
P_RE, P_IM = T_COS.T, -T_SIN.T

Y_IN = twice_table(np.stack([COS, SIN], 1).reshape(2 * K, N))
Y_OUT = wide(np.concatenate([COS, SIN], 0).T)
X_IN = wide(np.concatenate([COS, SIN], 0))
X_OUT = wide(np.concatenate([COS, SIN], 0).T)


def t_in():
    re = rounded(P_RE).astype(np.float64).reshape(TP, 2, K)
    im = rounded(P_IM).astype(np.float64).reshape(TP, 2, K)
    rows_re = np.concatenate([re, im], 0)
    rows_im = np.concatenate([im, -re], 0)
    both = np.stack([rows_re, rows_im], 0)
    table = both.transpose(0, 2, 3, 1).reshape(4 * K, 2 * TP)
    return rounded(np.concatenate([table, table], 1))


def t_out():
    re = P_RE.reshape(TP, 2, K)
    im = P_IM.reshape(TP, 2, K)
    of_c = np.stack([re, im], 2)
    of_s = np.stack([im, -re], 2)
    return wide(np.concatenate([of_c, of_s], 0).reshape(2 * TP, 4 * K))


TABLES = {
    "y_in": Y_IN,
    "t_in": t_in(),
    "y_out": Y_OUT,
    "x_in": X_IN,
    "x_out": X_OUT,
    "t_out": t_out(),
}
PLACES = {}
for name, values in TABLES.items():
    PLACES[name] = (sum(TABLES[other].shape[0] for other in PLACES), *values.shape)
PACKED = np.concatenate([np.pad(v, ((0, 0), (0, 256 - v.shape[1]))) for v in TABLES.values()], 0)


def table(ref, name):
    first, rows, columns = PLACES[name]
    return ref[first : first + rows, :columns]


def dot(left, right):
    return jnp.dot(left, right, preferred_element_type=F32)


def split(data):
    high = data.astype(BF)
    return high, (data - high.astype(F32)).astype(BF)


def stack3(data):
    high, low = split(data)
    return jnp.concatenate([high, high, low], 0)


def stack2(data):
    high, low = split(data)
    return jnp.concatenate([high, low], 0)


def low_lanes(shape):
    return lax.broadcasted_iota(jnp.int32, shape, 1) < C


def swap(data):
    return pltpu.roll(data, C, 1)


def turned(data):
    other = swap(data)
    return jnp.where(low_lanes(data.shape), -other, other)


def lanes(blocks):
    return jnp.concatenate(blocks, 1)


Y_TILES = 32


def y_analysis_store(chunk, first_tile, tiles, y_in, scratch):
    out = dot(y_in, jnp.concatenate([chunk, chunk], 0))
    scratch[:, first_tile : first_tile + tiles, :] = out.reshape(2 * K, tiles, 128)


def t_analysis(scratch, t_table, out_ref, x, group=16):
    low = low_lanes((K, 128))
    for first in range(0, K, group):
        data = lanes([scratch[2 * (first + j) : 2 * (first + j + 1)].reshape(2 * TP, 128) for j in range(group)])
        res = dot(t_table, stack2(data))
        for j in range(group):
            re0, re1, im0, im1 = (res[q * K : (q + 1) * K, j * 128 : (j + 1) * 128] for q in range(4))
            both = jnp.where(low, re0, im1) + swap(jnp.where(low, im0, re1))
            out_ref[2 * (first + j), x] = both[:8]
            out_ref[2 * (first + j) + 1, x] = both[8:]


def t_synthesis(w_ref, t_table, scratch, x, group=16):
    low = low_lanes((K, 128))
    zero = jnp.zeros((K, 128), F32)
    for first in range(0, K, group):
        blocks = []
        for j in range(group):
            w = jnp.concatenate([w_ref[2 * (first + j), x], w_ref[2 * (first + j) + 1, x]], 0)
            other = swap(w)
            blocks.append(
                jnp.concatenate(
                    [
                        jnp.where(low, w, zero),
                        jnp.where(low, other, zero),
                        jnp.where(low, zero, other),
                        jnp.where(low, zero, w),
                    ],
                    0,
                )
            )
        res = dot(t_table, stack3(lanes(blocks)))
        for cs in range(2):
            scratch[:, cs * K + first : cs * K + first + group, :] = res[cs * TP : (cs + 1) * TP].reshape(
                TP, group, 128
            )


def y_synthesis(scratch, first_tile, tiles, y_out):
    data = lanes(
        [
            scratch[first_tile + j]
            for j in range(tiles)
        ]
    )
    return dot(y_out, stack3(data))


def channel_map(chunk, weight, tiles, contracted=0):
    rows = jnp.concatenate([chunk[:, j * 128 : (j + 1) * 128] for j in range(tiles)], 0)
    out = lax.dot_general(
        rows, weight, (((1,), (contracted,)), ((), ())), preferred_element_type=F32
    )
    return lanes([out[j * N : (j + 1) * N] for j in range(tiles)])


def lane_slice(step, tiles):
    return pl.ds(step * tiles * 128, tiles * 128)


HALF = N * C // 2


def start_all(sems, *moves):
    copies = [pltpu.make_async_copy(*move, sems.at[i]) for i, move in enumerate(moves)]
    for copy in copies:
        copy.start()
    return copies


def analyse_kernel(
    field_in, w_in, tables_in, map_in, bias_in,
    out_ref, w_ref, tables_ref, map_ref, bias_ref,
    field, scratch, small_map, small_bias, sems,
):
    parts = [(i // 2, slice(None), pl.ds(i % 2 * HALF, HALF)) for i in range(2 * CX)]
    copies = start_all(
        sems,
        (tables_in, tables_ref),
        *((field_in.at[part], field.at[part]) for part in parts),
        (map_in, small_map),
        (bias_in, small_bias),
        (w_in, w_ref),
    )
    copies[0].wait()
    y_in, t_in = table(tables_ref, "y_in"), table(tables_ref, "t_in")
    for x in range(CX):
        copies[1 + 2 * x].wait()
        copies[2 + 2 * x].wait()
        y_analysis_store(field[x], 0, TP, y_in, scratch)
        t_analysis(scratch, t_in, out_ref, x)
    for copy in copies[1 + 2 * CX :]:
        copy.wait()
    wide_map = jnp.concatenate([small_map[...]] * 2, 1)
    wide_map = jnp.concatenate([wide_map] * 2, 0)
    row = lax.broadcasted_iota(jnp.int32, (2 * C, 2 * C), 0) // C
    lane = lax.broadcasted_iota(jnp.int32, (2 * C, 2 * C), 1) // C
    map_ref[...] = jnp.where(row == lane, wide_map, jnp.zeros_like(wide_map))
    bias_ref[...] = jnp.concatenate([small_bias[...]] * 2, 1)


def gelu_slope(z):
    square = z * z
    tanh_value = jnp.tanh(z * (SQRT_TWO_PI + SQRT_TWO_PI * 0.044715 * square))
    half_rise = z * (0.5 * SQRT_TWO_PI + 1.5 * SQRT_TWO_PI * 0.044715 * square)
    return (1.0 + tanh_value) * (0.5 + half_rise * (1.0 - tanh_value))


def middle_kernel(
    w_ref, field_in, cot_in, map_ref, bias_ref, tables_ref, gz_out, out_ref, field, cot, gz, syn, ana, sems
):
    copies = start_all(
        sems,
        (field_in.at[0], field.at[0]),
        (cot_in.at[0], cot.at[0]),
        (field_in.at[1], field.at[1]),
        (cot_in.at[1], cot.at[1]),
    )
    backs = [pltpu.make_async_copy(gz.at[x], gz_out.at[x], sems.at[len(copies) + x]) for x in range(CX)]
    y_in, y_out, t_in, t_out = (table(tables_ref, name) for name in ("y_in", "y_out", "t_in", "t_out"))
    for x in range(CX):
        t_synthesis(w_ref, t_out, syn.at[x], x)
    for x in range(CX):
        copies[2 * x].wait()
        copies[2 * x + 1].wait()

        for step in range(TP // Y_TILES):
            at = lane_slice(step, Y_TILES)
            spec = y_synthesis(syn.at[x], step * Y_TILES, Y_TILES, y_out)
            z = spec + channel_map(field[x, :, at], map_ref[...], Y_TILES) + lanes([bias_ref[...]] * Y_TILES)
            out = (cot[x, :, at].astype(F32) * gelu_slope(z)).astype(BF)
            gz[x, :, at] = out
            y_analysis_store(out, step * Y_TILES, Y_TILES, y_in, ana.at[x])

        backs[x].start()
    for x in range(CX):
        t_analysis(ana.at[x], t_in, out_ref, x)
    for back in backs:
        back.wait()


def final_kernel(w_ref, gz_in, map_ref, tables_ref, grad_out, gz, grad, syn, sems):
    copies = start_all(sems, (gz_in.at[0], gz.at[0]), (gz_in.at[1], gz.at[1]))
    backs = [
        pltpu.make_async_copy(grad.at[x], grad_out.at[x], sems.at[len(copies) + x]) for x in range(CX)
    ]
    y_out, t_out = table(tables_ref, "y_out"), table(tables_ref, "t_out")
    for x in range(CX):
        t_synthesis(w_ref, t_out, syn.at[x], x)
    for x in range(CX):
        copies[x].wait()

        for step in range(TP // Y_TILES):
            at = lane_slice(step, Y_TILES)
            spec = y_synthesis(syn.at[x], step * Y_TILES, Y_TILES, y_out)
            grad[x, :, at] = (spec + channel_map(gz[x, :, at], map_ref[...], Y_TILES, 1)).astype(BF)

        backs[x].start()
    for back in backs:
        back.wait()


M = 8


def x_analysis(in_ref, x_in):
    data = in_ref[...].reshape(N, M * 128)
    res = dot(x_in, stack3(data))
    out = []
    for m in range(M):
        cos_part = res[:K, m * 128 : (m + 1) * 128]
        sin_part = res[K:, m * 128 : (m + 1) * 128]
        out.append(cos_part - turned(sin_part))
    return out


def x_synthesis(blocks, x_out, out_ref):
    data = lanes([jnp.concatenate([v, turned(v)], 0) for v in blocks])
    res = dot(x_out, stack3(data))
    out_ref[...] = res.reshape(N, M, 128)


def mix(u, weights):
    low = low_lanes((K, 128))
    other = swap(u)
    rows = jnp.concatenate([jnp.where(low, u, other), jnp.where(low, other, u)], 0)
    parts = jnp.concatenate(split(rows), 0).astype(F32)
    row = lax.broadcasted_iota(jnp.int32, (4 * K, 128), 0) % K
    half = lax.broadcasted_iota(jnp.int32, (4 * K, 128), 1) // C
    left = lanes([jnp.where(row == 2 * j + half, parts, 0.0).astype(BF) for j in range(K // 2)])
    res = dot(left, weights)
    res = res[: 2 * K] + res[2 * K :]
    return res[:K] + turned(res[K:])


def mix_adjoint(g, weights):
    rows = jnp.concatenate([g, -turned(g)], 0)
    parts = jnp.concatenate(split(rows), 0)
    res = lax.dot_general(parts, weights, (((1,), (1,)), ((), ())), preferred_element_type=F32)
    res = res[: 2 * K] + res[2 * K :]
    row = lax.broadcasted_iota(jnp.int32, (2 * K, 128), 0) % K
    half = lax.broadcasted_iota(jnp.int32, (2 * K, 128), 1) // C
    total = jnp.zeros((2 * K, 128), F32)
    for j in range(K // 2):
        total = total + jnp.where(row == 2 * j + half, res[:, j * 128 : (j + 1) * 128], 0.0)
    total = total + swap(total)
    return jnp.where(low_lanes((K, 128)), total[:K], total[K:])


def mix_kernel(in_ref, w_ref, tables_ref, hat_ref, out_ref):
    spectra = x_analysis(in_ref, table(tables_ref, "x_in"))
    mixed = []
    for m in range(M):
        hat_ref[m] = spectra[m]
        mixed.append(mix(spectra[m], w_ref[m]))
    x_synthesis(mixed, table(tables_ref, "x_out"), out_ref)


def adjoint_kernel(in_ref, u_ref, w_ref, tables_ref, hats_ref, out_ref):
    spectra = x_analysis(in_ref, table(tables_ref, "x_in"))
    mixed = []
    for m in range(M):
        hats_ref[0, m] = u_ref[m]
        hats_ref[1, m] = spectra[m]
        mixed.append(mix_adjoint(spectra[m], w_ref[m]))
    x_synthesis(mixed, table(tables_ref, "x_out"), out_ref)


def grads_kernel(*refs):
    hats, (grads_out, grads, sems) = refs[:DP], refs[DP:]
    own = lax.broadcasted_iota(jnp.int32, (C, 2 * DP * K), 1) % K // 2
    odd = lax.broadcasted_iota(jnp.int32, (2 * DP * K, 1), 0) % 2 == 1
    copies = [pltpu.make_async_copy(grads.at[m], grads_out.at[m], sems.at[m]) for m in range(M)]
    for m in range(M):
        u, g = (jnp.concatenate([hat[i, m] for hat in hats], 0) for i in range(2))
        u_t = u.T.astype(BF)
        left = lanes([u_t[:C], u_t[C:]])
        right = jnp.concatenate([g, -turned(g)], 0)
        right = lanes([jnp.where(odd, 0.0, right), jnp.where(odd, right, 0.0)]).astype(BF)
        tall = jnp.concatenate([jnp.where(own == q, left, jnp.zeros_like(left)) for q in range(K // 2)], 0)
        out = dot(tall, right)
        for kx in range(K):
            grads[m, kx] = out[kx // 2 * C : (kx // 2 + 1) * C, kx % 2 * 128 : (kx % 2 + 1) * 128]
        copies[m].start()
    for copy in copies:
        copy.wait()


LIMIT = 32
IN_VMEM = pl.BlockSpec(memory_space=pltpu.VMEM)
IN_HBM = pl.BlockSpec(memory_space=pltpu.HBM)


def call(kernel, name, out_shapes, out_specs, scratch, *operands, specs):
    return pl.pallas_call(
        kernel,
        name=name,
        out_shape=out_shapes,
        in_specs=specs,
        out_specs=out_specs,
        scratch_shapes=scratch,
        compiler_params=pltpu.CompilerParams(vmem_limit_bytes=LIMIT * 2**20),
    )(*operands)


def in_vmem(*arrays):
    return [pltpu.with_memory_space_constraint(array, pltpu.VMEM) for array in arrays]


def in_hbm(*arrays):
    return [pltpu.with_memory_space_constraint(array, pltpu.HBM) for array in arrays]


def shape(dims, kind=F32):
    return jax.ShapeDtypeStruct(dims, kind)


SPECTRA = shape((SLABS, CX, M, 128))
BOTH_ROWS = pltpu.VMEM((CX, 2 * K, TP, 128), F32)
ROWS = pltpu.VMEM((2 * K, TP, 128), F32)


def exchange(data):
    return lax.all_to_all(data, "slab", 0, 0, tiled=True)


Y_RING = 4


def x_partner(data):
    return lax.ppermute(data, "dp", [(i, (i + Y_RING) % DP) for i in range(DP)])


def y_neighbours(data):
    return [
        lax.ppermute(data, "dp", [(i, i // Y_RING * Y_RING + (i + by) % Y_RING) for i in range(DP)])
        for by in (2, 3, 1)
    ]


def body(field, cotangent, mode_weights, w_local, bias):
    grid_shape = (CX, N, N * C)
    on_grid = pltpu.VMEM(grid_shape, BF)
    values, cot = field.reshape(grid_shape), cotangent.reshape(grid_shape)

    first, weights, tables, wide_map, wide_bias = call(
        analyse_kernel,
        "analyse",
        (
            SPECTRA,
            pltpu.VMEM((M, K * C, 2 * C), BF),
            pltpu.VMEM(PACKED.shape, BF),
            pltpu.VMEM((2 * C, 2 * C), BF),
            pltpu.VMEM((1, 2 * C), F32),
        ),
        [IN_VMEM] * 5,
        [on_grid, ROWS, pltpu.VMEM((C, C), BF), pltpu.VMEM((1, C), F32), pltpu.SemaphoreType.DMA((8,))],
        *in_hbm(
            values, mode_weights.reshape(M, K * C, 2 * C), jnp.asarray(PACKED), w_local, bias.reshape(1, C)
        ),
        specs=[IN_HBM] * 5,
    )
    u_hat, mixed = call(
        mix_kernel,
        "mix",
        (shape((M, K, 128)), shape((N, M, 128))),
        [IN_VMEM] * 2,
        [],
        exchange(first).reshape(N, M, 128),
        *in_vmem(weights, tables),
        specs=[IN_VMEM] * 3,
    )
    arrived = exchange(mixed.reshape(SPECTRA.shape))
    gz, second = call(
        middle_kernel,
        "middle",
        (pltpu.HBM(grid_shape, BF), SPECTRA),
        [IN_HBM, IN_VMEM],
        [on_grid, on_grid, on_grid, BOTH_ROWS, BOTH_ROWS, pltpu.SemaphoreType.DMA((6,))],
        arrived,
        *in_hbm(values, cot),
        *in_vmem(wide_map, wide_bias, tables),
        specs=[IN_VMEM] + [IN_HBM] * 2 + [IN_VMEM] * 3,
    )
    hats, back = call(
        adjoint_kernel,
        "adjoint",
        (shape((2, M, K, 128)), shape((N, M, 128))),
        [IN_VMEM] * 2,
        [],
        exchange(second).reshape(N, M, 128),
        u_hat,
        *in_vmem(weights, tables),
        specs=[IN_VMEM] * 4,
    )
    partner = x_partner(hats)
    opposite, back_one, next_one = y_neighbours(hats)
    others = [opposite, back_one, next_one, partner, x_partner(opposite), *y_neighbours(partner)[1:]]
    grad_field = call(
        final_kernel,
        "final",
        pltpu.HBM(grid_shape, BF),
        IN_HBM,
        [on_grid, on_grid, BOTH_ROWS, pltpu.SemaphoreType.DMA((4,))],
        exchange(back.reshape(SPECTRA.shape)),
        *in_hbm(gz),
        *in_vmem(wide_map, tables),
        specs=[IN_VMEM, IN_HBM] + [IN_VMEM] * 2,
    )
    grad_field, *others = lax.optimization_barrier((grad_field, *others))
    grad_modes = call(
        grads_kernel,
        "weight_grads",
        pltpu.HBM((M, K, C, 2 * C), F32),
        IN_HBM,
        [pltpu.VMEM((M, K, C, 2 * C), F32), pltpu.SemaphoreType.DMA((M,))],
        hats,
        *others,
        specs=[IN_VMEM] * DP,
    )
    return grad_field.reshape(field.shape), grad_modes


def solution(mesh):
    placed = (
        P("dp", "slab", None, None),
        P("dp", "slab", None, None),
        P("slab", None, None, None),
        P(),
        P(),
    )
    return jax.shard_map(
        body,
        mesh=mesh,
        in_specs=placed,
        out_specs=(P("dp", "slab", None, None), P("slab", None, None, None)),
        check_vma=False,
    )
```

```python
import math

import jax
import jax.numpy as jnp
import ml_dtypes
import numpy as np
from jax import lax
from jax.experimental import pallas as pl
from jax.experimental.pallas import tpu as pltpu
from jax.sharding import PartitionSpec as P

C = 64
K = 16
N = 64
CX = 2
SLABS = 32
DP = 8
TP = N // 2

BF = jnp.bfloat16
F32 = jnp.float32
SQRT_TWO_PI = math.sqrt(2.0 / math.pi)


def trig(freqs):
    phase = (freqs[:, None] * np.arange(N)[None, :] % N) * (2.0 * math.pi / N)
    return np.cos(phase) / math.sqrt(N), np.sin(phase) / math.sqrt(N)


def rounded(table):
    return table.astype(np.float32).astype(ml_dtypes.bfloat16)


def wide(table):
    high = rounded(table)
    low = rounded(table - high.astype(np.float64))
    return np.concatenate([high, low, high], 1)


def twice_table(table):
    high = rounded(table)
    low = rounded(table - high.astype(np.float64))
    return np.concatenate([high, low], 1)


SIGNED = np.concatenate([np.arange(K // 2), np.arange(-K // 2, 0)])
COS, SIN = trig(SIGNED)
T_COS, T_SIN = trig(np.arange(K))
P_RE, P_IM = T_COS.T, -T_SIN.T

Y_IN = twice_table(np.stack([COS, SIN], 1).reshape(2 * K, N))
Y_OUT = wide(np.concatenate([COS, SIN], 0).T)
X_IN = wide(np.concatenate([COS, SIN], 0))
X_OUT = wide(np.concatenate([COS, SIN], 0).T)


def t_in():
    re = rounded(P_RE).astype(np.float64).reshape(TP, 2, K)
    im = rounded(P_IM).astype(np.float64).reshape(TP, 2, K)
    rows_re = np.concatenate([re, im], 0)
    rows_im = np.concatenate([im, -re], 0)
    both = np.stack([rows_re, rows_im], 0)
    table = both.transpose(0, 2, 3, 1).reshape(4 * K, 2 * TP)
    return rounded(np.concatenate([table, table], 1))


def t_out():
    re = P_RE.reshape(TP, 2, K)
    im = P_IM.reshape(TP, 2, K)
    of_c = np.stack([re, im], 2)
    of_s = np.stack([im, -re], 2)
    return wide(np.concatenate([of_c, of_s], 0).reshape(2 * TP, 4 * K))


TABLES = {
    "y_in": Y_IN,
    "t_in": t_in(),
    "y_out": Y_OUT,
    "x_in": X_IN,
    "x_out": X_OUT,
    "t_out": t_out(),
}
PLACES = {}
for name, values in TABLES.items():
    PLACES[name] = (sum(TABLES[other].shape[0] for other in PLACES), *values.shape)
PACKED = np.concatenate([np.pad(v, ((0, 0), (0, 256 - v.shape[1]))) for v in TABLES.values()], 0)


def table(ref, name):
    first, rows, columns = PLACES[name]
    return ref[first : first + rows, :columns]


def dot(left, right):
    return jnp.dot(left, right, preferred_element_type=F32)


def split(data):
    high = data.astype(BF)
    return high, (data - high.astype(F32)).astype(BF)


def stack3(data):
    high, low = split(data)
    return jnp.concatenate([high, high, low], 0)


def stack2(data):
    high, low = split(data)
    return jnp.concatenate([high, low], 0)


def low_lanes(shape):
    return lax.broadcasted_iota(jnp.int32, shape, 1) < C


def swap(data):
    return pltpu.roll(data, C, 1)


def turned(data):
    other = swap(data)
    return jnp.where(low_lanes(data.shape), -other, other)


def lanes(blocks):
    return jnp.concatenate(blocks, 1)


Y_TILES = 32


def y_analysis_store(chunk, first_tile, tiles, y_in, scratch):
    out = dot(y_in, jnp.concatenate([chunk, chunk], 0))
    scratch[:, first_tile : first_tile + tiles, :] = out.reshape(2 * K, tiles, 128)


def t_analysis(scratch, t_table, out_ref, x, group=16):
    low = low_lanes((K, 128))
    for first in range(0, K, group):
        data = lanes([scratch[2 * (first + j) : 2 * (first + j + 1)].reshape(2 * TP, 128) for j in range(group)])
        res = dot(t_table, stack2(data))
        for j in range(group):
            re0, re1, im0, im1 = (res[q * K : (q + 1) * K, j * 128 : (j + 1) * 128] for q in range(4))
            both = jnp.where(low, re0, im1) + swap(jnp.where(low, im0, re1))
            out_ref[2 * (first + j), x] = both[:8]
            out_ref[2 * (first + j) + 1, x] = both[8:]


def t_synthesis(w_ref, t_table, scratch, x, group=16):
    low = low_lanes((K, 128))
    zero = jnp.zeros((K, 128), F32)
    for first in range(0, K, group):
        blocks = []
        for j in range(group):
            w = jnp.concatenate([w_ref[2 * (first + j), x], w_ref[2 * (first + j) + 1, x]], 0)
            other = swap(w)
            blocks.append(
                jnp.concatenate(
                    [
                        jnp.where(low, w, zero),
                        jnp.where(low, other, zero),
                        jnp.where(low, zero, other),
                        jnp.where(low, zero, w),
                    ],
                    0,
                )
            )
        res = dot(t_table, stack3(lanes(blocks)))
        for cs in range(2):
            scratch[:, cs * K + first : cs * K + first + group, :] = res[cs * TP : (cs + 1) * TP].reshape(
                TP, group, 128
            )


def y_synthesis(scratch, first_tile, tiles, y_out):
    data = lanes(
        [
            scratch[first_tile + j]
            for j in range(tiles)
        ]
    )
    return dot(y_out, stack3(data))


def channel_map(chunk, weight, tiles, contracted=0):
    rows = jnp.concatenate([chunk[:, j * 128 : (j + 1) * 128] for j in range(tiles)], 0)
    out = lax.dot_general(
        rows, weight, (((1,), (contracted,)), ((), ())), preferred_element_type=F32
    )
    return lanes([out[j * N : (j + 1) * N] for j in range(tiles)])


def lane_slice(step, tiles):
    return pl.ds(step * tiles * 128, tiles * 128)


HALF = N * C // 2


def start_all(sems, *moves):
    copies = [pltpu.make_async_copy(*move, sems.at[i]) for i, move in enumerate(moves)]
    for copy in copies:
        copy.start()
    return copies


def analyse_kernel(
    field_in, w_in, tables_in, map_in, bias_in,
    out_ref, w_ref, tables_ref, map_ref, bias_ref,
    field, scratch, small_map, small_bias, sems,
):
    parts = [(i // 2, slice(None), pl.ds(i % 2 * HALF, HALF)) for i in range(2 * CX)]
    copies = start_all(
        sems,
        (tables_in, tables_ref),
        *((field_in.at[part], field.at[part]) for part in parts),
        (map_in, small_map),
        (bias_in, small_bias),
        (w_in, w_ref),
    )
    copies[0].wait()
    y_in, t_in = table(tables_ref, "y_in"), table(tables_ref, "t_in")
    for x in range(CX):
        copies[1 + 2 * x].wait()
        copies[2 + 2 * x].wait()
        y_analysis_store(field[x], 0, TP, y_in, scratch)
        t_analysis(scratch, t_in, out_ref, x)
    for copy in copies[1 + 2 * CX :]:
        copy.wait()
    wide_map = jnp.concatenate([small_map[...]] * 2, 1)
    wide_map = jnp.concatenate([wide_map] * 2, 0)
    row = lax.broadcasted_iota(jnp.int32, (2 * C, 2 * C), 0) // C
    lane = lax.broadcasted_iota(jnp.int32, (2 * C, 2 * C), 1) // C
    map_ref[...] = jnp.where(row == lane, wide_map, jnp.zeros_like(wide_map))
    bias_ref[...] = jnp.concatenate([small_bias[...]] * 2, 1)


def gelu_slope(z):
    square = z * z
    tanh_value = jnp.tanh(z * (SQRT_TWO_PI + SQRT_TWO_PI * 0.044715 * square))
    half_rise = z * (0.5 * SQRT_TWO_PI + 1.5 * SQRT_TWO_PI * 0.044715 * square)
    return (1.0 + tanh_value) * (0.5 + half_rise * (1.0 - tanh_value))


def middle_kernel(
    w_ref, field, cot, map_ref, bias_ref, tables_ref, gz_out, out_ref, gz, syn, ana, sems
):
    backs = [pltpu.make_async_copy(gz.at[x], gz_out.at[x], sems.at[x]) for x in range(CX)]
    y_in, y_out, t_in, t_out = (table(tables_ref, name) for name in ("y_in", "y_out", "t_in", "t_out"))
    for x in range(CX):
        t_synthesis(w_ref, t_out, syn.at[x], x)
    for x in range(CX):

        for step in range(TP // Y_TILES):
            at = lane_slice(step, Y_TILES)
            spec = y_synthesis(syn.at[x], step * Y_TILES, Y_TILES, y_out)
            z = spec + channel_map(field[x, :, at], map_ref[...], Y_TILES) + lanes([bias_ref[...]] * Y_TILES)
            out = (cot[x, :, at].astype(F32) * gelu_slope(z)).astype(BF)
            gz[x, :, at] = out
            y_analysis_store(out, step * Y_TILES, Y_TILES, y_in, ana.at[x])

        backs[x].start()
    for x in range(CX):
        t_analysis(ana.at[x], t_in, out_ref, x)
    for back in backs:
        back.wait()


def final_kernel(w_ref, gz, map_ref, tables_ref, grad_out, grad, syn, sems):
    backs = [pltpu.make_async_copy(grad.at[x], grad_out.at[x], sems.at[x]) for x in range(CX)]
    y_out, t_out = table(tables_ref, "y_out"), table(tables_ref, "t_out")
    for x in range(CX):
        t_synthesis(w_ref, t_out, syn.at[x], x)
    for x in range(CX):

        for step in range(TP // Y_TILES):
            at = lane_slice(step, Y_TILES)
            spec = y_synthesis(syn.at[x], step * Y_TILES, Y_TILES, y_out)
            grad[x, :, at] = (spec + channel_map(gz[x, :, at], map_ref[...], Y_TILES, 1)).astype(BF)

        backs[x].start()
    for back in backs:
        back.wait()


M = 8


def x_analysis(in_ref, x_in):
    data = in_ref[...].reshape(N, M * 128)
    res = dot(x_in, stack3(data))
    out = []
    for m in range(M):
        cos_part = res[:K, m * 128 : (m + 1) * 128]
        sin_part = res[K:, m * 128 : (m + 1) * 128]
        out.append(cos_part - turned(sin_part))
    return out


def x_synthesis(blocks, x_out, out_ref):
    data = lanes([jnp.concatenate([v, turned(v)], 0) for v in blocks])
    res = dot(x_out, stack3(data))
    out_ref[...] = res.reshape(N, M, 128)


def mix(u, weights):
    low = low_lanes((K, 128))
    other = swap(u)
    rows = jnp.concatenate([jnp.where(low, u, other), jnp.where(low, other, u)], 0)
    parts = jnp.concatenate(split(rows), 0).astype(F32)
    row = lax.broadcasted_iota(jnp.int32, (4 * K, 128), 0) % K
    half = lax.broadcasted_iota(jnp.int32, (4 * K, 128), 1) // C
    left = lanes([jnp.where(row == 2 * j + half, parts, 0.0).astype(BF) for j in range(K // 2)])
    res = dot(left, weights)
    res = res[: 2 * K] + res[2 * K :]
    return res[:K] + turned(res[K:])


def mix_adjoint(g, weights):
    rows = jnp.concatenate([g, -turned(g)], 0)
    parts = jnp.concatenate(split(rows), 0)
    res = lax.dot_general(parts, weights, (((1,), (1,)), ((), ())), preferred_element_type=F32)
    res = res[: 2 * K] + res[2 * K :]
    row = lax.broadcasted_iota(jnp.int32, (2 * K, 128), 0) % K
    half = lax.broadcasted_iota(jnp.int32, (2 * K, 128), 1) // C
    total = jnp.zeros((2 * K, 128), F32)
    for j in range(K // 2):
        total = total + jnp.where(row == 2 * j + half, res[:, j * 128 : (j + 1) * 128], 0.0)
    total = total + swap(total)
    return jnp.where(low_lanes((K, 128)), total[:K], total[K:])


def mix_kernel(in_ref, w_ref, tables_ref, hat_ref, out_ref):
    spectra = x_analysis(in_ref, table(tables_ref, "x_in"))
    mixed = []
    for m in range(M):
        hat_ref[m] = spectra[m]
        mixed.append(mix(spectra[m], w_ref[m]))
    x_synthesis(mixed, table(tables_ref, "x_out"), out_ref)


def adjoint_kernel(in_ref, u_ref, w_ref, tables_ref, hats_ref, out_ref):
    spectra = x_analysis(in_ref, table(tables_ref, "x_in"))
    mixed = []
    for m in range(M):
        hats_ref[0, m] = u_ref[m]
        hats_ref[1, m] = spectra[m]
        mixed.append(mix_adjoint(spectra[m], w_ref[m]))
    x_synthesis(mixed, table(tables_ref, "x_out"), out_ref)


def grads_kernel(*refs):
    hats, (grads_out, grads, sems) = refs[:DP], refs[DP:]
    own = lax.broadcasted_iota(jnp.int32, (C, 2 * DP * K), 1) % K // 2
    odd = lax.broadcasted_iota(jnp.int32, (2 * DP * K, 1), 0) % 2 == 1
    copies = [pltpu.make_async_copy(grads.at[m], grads_out.at[m], sems.at[m]) for m in range(M)]
    for m in range(M):
        u, g = (jnp.concatenate([hat[i, m] for hat in hats], 0) for i in range(2))
        u_t = u.T.astype(BF)
        left = lanes([u_t[:C], u_t[C:]])
        right = jnp.concatenate([g, -turned(g)], 0)
        right = lanes([jnp.where(odd, 0.0, right), jnp.where(odd, right, 0.0)]).astype(BF)
        tall = jnp.concatenate([jnp.where(own == q, left, jnp.zeros_like(left)) for q in range(K // 2)], 0)
        out = dot(tall, right)
        for kx in range(K):
            grads[m, kx] = out[kx // 2 * C : (kx // 2 + 1) * C, kx % 2 * 128 : (kx % 2 + 1) * 128]
        copies[m].start()
    for copy in copies:
        copy.wait()


LIMIT = 32
IN_VMEM = pl.BlockSpec(memory_space=pltpu.VMEM)
IN_HBM = pl.BlockSpec(memory_space=pltpu.HBM)


def call(kernel, name, out_shapes, out_specs, scratch, *operands, specs):
    return pl.pallas_call(
        kernel,
        name=name,
        out_shape=out_shapes,
        in_specs=specs,
        out_specs=out_specs,
        scratch_shapes=scratch,
        compiler_params=pltpu.CompilerParams(vmem_limit_bytes=LIMIT * 2**20),
    )(*operands)


def in_vmem(*arrays):
    return [pltpu.with_memory_space_constraint(array, pltpu.VMEM) for array in arrays]


def in_hbm(*arrays):
    return [pltpu.with_memory_space_constraint(array, pltpu.HBM) for array in arrays]


def shape(dims, kind=F32):
    return jax.ShapeDtypeStruct(dims, kind)


SPECTRA = shape((SLABS, CX, M, 128))
BOTH_ROWS = pltpu.VMEM((CX, 2 * K, TP, 128), F32)
ROWS = pltpu.VMEM((2 * K, TP, 128), F32)


def exchange(data):
    return lax.all_to_all(data, "slab", 0, 0, tiled=True)


Y_RING = 4


def x_partner(data):
    return lax.ppermute(data, "dp", [(i, (i + Y_RING) % DP) for i in range(DP)])


def y_neighbours(data):
    return [
        lax.ppermute(data, "dp", [(i, i // Y_RING * Y_RING + (i + by) % Y_RING) for i in range(DP)])
        for by in (2, 3, 1)
    ]


def body(field, cotangent, mode_weights, w_local, bias):
    grid_shape = (CX, N, N * C)
    on_grid = pltpu.VMEM(grid_shape, BF)
    values, cot = field.reshape(grid_shape), cotangent.reshape(grid_shape)

    first, weights, tables, wide_map, wide_bias = call(
        analyse_kernel,
        "analyse",
        (
            SPECTRA,
            pltpu.VMEM((M, K * C, 2 * C), BF),
            pltpu.VMEM(PACKED.shape, BF),
            pltpu.VMEM((2 * C, 2 * C), BF),
            pltpu.VMEM((1, 2 * C), F32),
        ),
        [IN_VMEM] * 5,
        [on_grid, ROWS, pltpu.VMEM((C, C), BF), pltpu.VMEM((1, C), F32), pltpu.SemaphoreType.DMA((8,))],
        *in_hbm(
            values, mode_weights.reshape(M, K * C, 2 * C), jnp.asarray(PACKED), w_local, bias.reshape(1, C)
        ),
        specs=[IN_HBM] * 5,
    )
    u_hat, mixed = call(
        mix_kernel,
        "mix",
        (shape((M, K, 128)), shape((N, M, 128))),
        [IN_VMEM] * 2,
        [],
        exchange(first).reshape(N, M, 128),
        *in_vmem(weights, tables),
        specs=[IN_VMEM] * 3,
    )
    arrived = exchange(mixed.reshape(SPECTRA.shape))
    gz, second = call(
        middle_kernel,
        "middle",
        (pltpu.HBM(grid_shape, BF), SPECTRA),
        [IN_HBM, IN_VMEM],
        [on_grid, BOTH_ROWS, BOTH_ROWS, pltpu.SemaphoreType.DMA((2,))],
        arrived,
        *in_vmem(values, cot, wide_map, wide_bias, tables),
        specs=[IN_VMEM] * 6,
    )
    hats, back = call(
        adjoint_kernel,
        "adjoint",
        (shape((2, M, K, 128)), shape((N, M, 128))),
        [IN_VMEM] * 2,
        [],
        exchange(second).reshape(N, M, 128),
        u_hat,
        *in_vmem(weights, tables),
        specs=[IN_VMEM] * 4,
    )
    partner = x_partner(hats)
    opposite, back_one, next_one = y_neighbours(hats)
    others = [opposite, back_one, next_one, partner, x_partner(opposite), *y_neighbours(partner)[1:]]
    grad_field = call(
        final_kernel,
        "final",
        pltpu.HBM(grid_shape, BF),
        IN_HBM,
        [on_grid, BOTH_ROWS, pltpu.SemaphoreType.DMA((2,))],
        exchange(back.reshape(SPECTRA.shape)),
        *in_vmem(gz, wide_map, tables),
        specs=[IN_VMEM] * 4,
    )
    grad_field, *others = lax.optimization_barrier((grad_field, *others))
    grad_modes = call(
        grads_kernel,
        "weight_grads",
        pltpu.HBM((M, K, C, 2 * C), F32),
        IN_HBM,
        [pltpu.VMEM((M, K, C, 2 * C), F32), pltpu.SemaphoreType.DMA((M,))],
        hats,
        *others,
        specs=[IN_VMEM] * DP,
    )
    return grad_field.reshape(field.shape), grad_modes


def solution(mesh):
    placed = (
        P("dp", "slab", None, None),
        P("dp", "slab", None, None),
        P("slab", None, None, None),
        P(),
        P(),
    )
    return jax.shard_map(
        body,
        mesh=mesh,
        in_specs=placed,
        out_specs=(P("dp", "slab", None, None), P("slab", None, None, None)),
        check_vma=False,
    )
```

```python
import math

import jax
import jax.numpy as jnp
import ml_dtypes
import numpy as np
from jax import lax
from jax.experimental import pallas as pl
from jax.experimental.pallas import tpu as pltpu
from jax.sharding import PartitionSpec as P

C = 64
K = 16
N = 64
CX = 2
SLABS = 32
DP = 8
TP = N // 2

BF = jnp.bfloat16
F32 = jnp.float32
SQRT_TWO_PI = math.sqrt(2.0 / math.pi)


def trig(freqs):
    phase = (freqs[:, None] * np.arange(N)[None, :] % N) * (2.0 * math.pi / N)
    return np.cos(phase) / math.sqrt(N), np.sin(phase) / math.sqrt(N)


def rounded(table):
    return table.astype(np.float32).astype(ml_dtypes.bfloat16)


def wide(table):
    high = rounded(table)
    low = rounded(table - high.astype(np.float64))
    return np.concatenate([high, low, high], 1)


def twice_table(table):
    high = rounded(table)
    low = rounded(table - high.astype(np.float64))
    return np.concatenate([high, low], 1)


SIGNED = np.concatenate([np.arange(K // 2), np.arange(-K // 2, 0)])
COS, SIN = trig(SIGNED)
T_COS, T_SIN = trig(np.arange(K))
P_RE, P_IM = T_COS.T, -T_SIN.T

Y_IN = twice_table(np.stack([COS, SIN], 1).reshape(2 * K, N))
Y_OUT = wide(np.concatenate([COS, SIN], 0).T)
X_IN = wide(np.concatenate([COS, SIN], 0))
X_OUT = wide(np.concatenate([COS, SIN], 0).T)


def t_in():
    re = rounded(P_RE).astype(np.float64).reshape(TP, 2, K)
    im = rounded(P_IM).astype(np.float64).reshape(TP, 2, K)
    rows_re = np.concatenate([re, im], 0)
    rows_im = np.concatenate([im, -re], 0)
    both = np.stack([rows_re, rows_im], 0)
    table = both.transpose(0, 2, 3, 1).reshape(4 * K, 2 * TP)
    return rounded(np.concatenate([table, table], 1))


def t_out():
    re = P_RE.reshape(TP, 2, K)
    im = P_IM.reshape(TP, 2, K)
    of_c = np.stack([re, im], 2)
    of_s = np.stack([im, -re], 2)
    return wide(np.concatenate([of_c, of_s], 0).reshape(2 * TP, 4 * K))


TABLES = {
    "y_in": Y_IN,
    "t_in": t_in(),
    "y_out": Y_OUT,
    "x_in": X_IN,
    "x_out": X_OUT,
    "t_out": t_out(),
}
PLACES = {}
for name, values in TABLES.items():
    PLACES[name] = (sum(TABLES[other].shape[0] for other in PLACES), *values.shape)
PACKED = np.concatenate([np.pad(v, ((0, 0), (0, 256 - v.shape[1]))) for v in TABLES.values()], 0)


def table(ref, name):
    first, rows, columns = PLACES[name]
    return ref[first : first + rows, :columns]


def dot(left, right):
    return jnp.dot(left, right, preferred_element_type=F32)


def split(data):
    high = data.astype(BF)
    return high, (data - high.astype(F32)).astype(BF)


def stack3(data):
    high, low = split(data)
    return jnp.concatenate([high, high, low], 0)


def stack2(data):
    high, low = split(data)
    return jnp.concatenate([high, low], 0)


def low_lanes(shape):
    return lax.broadcasted_iota(jnp.int32, shape, 1) < C


def swap(data):
    return pltpu.roll(data, C, 1)


def turned(data):
    other = swap(data)
    return jnp.where(low_lanes(data.shape), -other, other)


def lanes(blocks):
    return jnp.concatenate(blocks, 1)


Y_TILES = 32


def y_analysis_store(chunk, first_tile, tiles, y_in, scratch):
    out = dot(y_in, jnp.concatenate([chunk, chunk], 0))
    scratch[:, first_tile : first_tile + tiles, :] = out.reshape(2 * K, tiles, 128)


def t_analysis(scratch, t_table, out_ref, x, group=16):
    low = low_lanes((K, 128))
    for first in range(0, K, group):
        data = lanes([scratch[2 * (first + j) : 2 * (first + j + 1)].reshape(2 * TP, 128) for j in range(group)])
        res = dot(t_table, stack2(data))
        for j in range(group):
            re0, re1, im0, im1 = (res[q * K : (q + 1) * K, j * 128 : (j + 1) * 128] for q in range(4))
            both = jnp.where(low, re0, im1) + swap(jnp.where(low, im0, re1))
            out_ref[2 * (first + j), x] = both[:8]
            out_ref[2 * (first + j) + 1, x] = both[8:]


def t_synthesis(w_ref, t_table, scratch, x, group=16):
    low = low_lanes((K, 128))
    zero = jnp.zeros((K, 128), F32)
    for first in range(0, K, group):
        blocks = []
        for j in range(group):
            w = jnp.concatenate([w_ref[2 * (first + j), x], w_ref[2 * (first + j) + 1, x]], 0)
            other = swap(w)
            blocks.append(
                jnp.concatenate(
                    [
                        jnp.where(low, w, zero),
                        jnp.where(low, other, zero),
                        jnp.where(low, zero, other),
                        jnp.where(low, zero, w),
                    ],
                    0,
                )
            )
        res = dot(t_table, stack3(lanes(blocks)))
        for cs in range(2):
            scratch[:, cs * K + first : cs * K + first + group, :] = res[cs * TP : (cs + 1) * TP].reshape(
                TP, group, 128
            )


def y_synthesis(scratch, first_tile, tiles, y_out):
    data = lanes(
        [
            scratch[first_tile + j]
            for j in range(tiles)
        ]
    )
    return dot(y_out, stack3(data))


def channel_map(chunk, weight, tiles, contracted=0):
    rows = jnp.concatenate([chunk[:, j * 128 : (j + 1) * 128] for j in range(tiles)], 0)
    out = lax.dot_general(
        rows, weight, (((1,), (contracted,)), ((), ())), preferred_element_type=F32
    )
    return lanes([out[j * N : (j + 1) * N] for j in range(tiles)])


def lane_slice(step, tiles):
    return pl.ds(step * tiles * 128, tiles * 128)


HALF = N * C // 2


def start_all(sems, *moves):
    copies = [pltpu.make_async_copy(*move, sems.at[i]) for i, move in enumerate(moves)]
    for copy in copies:
        copy.start()
    return copies


def analyse_kernel(
    field_in, w_in, tables_in, map_in, bias_in,
    out_ref, w_ref, tables_ref, map_ref, bias_ref,
    field, scratch, small_map, small_bias, sems,
):
    parts = [(i // 2, slice(None), pl.ds(i % 2 * HALF, HALF)) for i in range(2 * CX)]
    copies = start_all(
        sems,
        (tables_in, tables_ref),
        *((field_in.at[part], field.at[part]) for part in parts),
        (map_in, small_map),
        (bias_in, small_bias),
        (w_in, w_ref),
    )
    copies[0].wait()
    y_in, t_in = table(tables_ref, "y_in"), table(tables_ref, "t_in")
    for x in range(CX):
        copies[1 + 2 * x].wait()
        copies[2 + 2 * x].wait()
        y_analysis_store(field[x], 0, TP, y_in, scratch.at[x])
    for x in range(CX):
        t_analysis(scratch.at[x], t_in, out_ref, x)
    for copy in copies[1 + 2 * CX :]:
        copy.wait()
    wide_map = jnp.concatenate([small_map[...]] * 2, 1)
    wide_map = jnp.concatenate([wide_map] * 2, 0)
    row = lax.broadcasted_iota(jnp.int32, (2 * C, 2 * C), 0) // C
    lane = lax.broadcasted_iota(jnp.int32, (2 * C, 2 * C), 1) // C
    map_ref[...] = jnp.where(row == lane, wide_map, jnp.zeros_like(wide_map))
    bias_ref[...] = jnp.concatenate([small_bias[...]] * 2, 1)


def gelu_slope(z):
    square = z * z
    tanh_value = jnp.tanh(z * (SQRT_TWO_PI + SQRT_TWO_PI * 0.044715 * square))
    half_rise = z * (0.5 * SQRT_TWO_PI + 1.5 * SQRT_TWO_PI * 0.044715 * square)
    return (1.0 + tanh_value) * (0.5 + half_rise * (1.0 - tanh_value))


def middle_kernel(
    w_ref, field, cot, map_ref, bias_ref, tables_ref, gz_out, out_ref, gz, syn, ana, sems
):
    backs = [pltpu.make_async_copy(gz.at[x], gz_out.at[x], sems.at[x]) for x in range(CX)]
    y_in, y_out, t_in, t_out = (table(tables_ref, name) for name in ("y_in", "y_out", "t_in", "t_out"))
    for x in range(CX):
        t_synthesis(w_ref, t_out, syn.at[x], x)
    for x in range(CX):

        for step in range(TP // Y_TILES):
            at = lane_slice(step, Y_TILES)
            spec = y_synthesis(syn.at[x], step * Y_TILES, Y_TILES, y_out)
            z = spec + channel_map(field[x, :, at], map_ref[...], Y_TILES) + lanes([bias_ref[...]] * Y_TILES)
            out = (cot[x, :, at].astype(F32) * gelu_slope(z)).astype(BF)
            gz[x, :, at] = out
            y_analysis_store(out, step * Y_TILES, Y_TILES, y_in, ana.at[x])

        backs[x].start()
    for x in range(CX):
        t_analysis(ana.at[x], t_in, out_ref, x)
    for back in backs:
        back.wait()


def final_kernel(w_ref, gz, map_ref, tables_ref, grad_out, grad, syn, sems):
    backs = [pltpu.make_async_copy(grad.at[x], grad_out.at[x], sems.at[x]) for x in range(CX)]
    y_out, t_out = table(tables_ref, "y_out"), table(tables_ref, "t_out")
    for x in range(CX):
        t_synthesis(w_ref, t_out, syn.at[x], x)
    for x in range(CX):

        for step in range(TP // Y_TILES):
            at = lane_slice(step, Y_TILES)
            spec = y_synthesis(syn.at[x], step * Y_TILES, Y_TILES, y_out)
            grad[x, :, at] = (spec + channel_map(gz[x, :, at], map_ref[...], Y_TILES, 1)).astype(BF)

        backs[x].start()
    for back in backs:
        back.wait()


M = 8


def x_analysis(in_ref, x_in):
    data = in_ref[...].reshape(N, M * 128)
    res = dot(x_in, stack3(data))
    out = []
    for m in range(M):
        cos_part = res[:K, m * 128 : (m + 1) * 128]
        sin_part = res[K:, m * 128 : (m + 1) * 128]
        out.append(cos_part - turned(sin_part))
    return out


def x_synthesis(blocks, x_out, out_ref):
    data = lanes([jnp.concatenate([v, turned(v)], 0) for v in blocks])
    res = dot(x_out, stack3(data))
    out_ref[...] = res.reshape(N, M, 128)


def mix(u, weights):
    low = low_lanes((K, 128))
    other = swap(u)
    rows = jnp.concatenate([jnp.where(low, u, other), jnp.where(low, other, u)], 0)
    parts = jnp.concatenate(split(rows), 0).astype(F32)
    row = lax.broadcasted_iota(jnp.int32, (4 * K, 128), 0) % K
    half = lax.broadcasted_iota(jnp.int32, (4 * K, 128), 1) // C
    left = lanes([jnp.where(row == 2 * j + half, parts, 0.0).astype(BF) for j in range(K // 2)])
    res = dot(left, weights)
    res = res[: 2 * K] + res[2 * K :]
    return res[:K] + turned(res[K:])


def mix_adjoint(g, weights):
    rows = jnp.concatenate([g, -turned(g)], 0)
    parts = jnp.concatenate(split(rows), 0)
    res = lax.dot_general(parts, weights, (((1,), (1,)), ((), ())), preferred_element_type=F32)
    res = res[: 2 * K] + res[2 * K :]
    row = lax.broadcasted_iota(jnp.int32, (2 * K, 128), 0) % K
    half = lax.broadcasted_iota(jnp.int32, (2 * K, 128), 1) // C
    total = jnp.zeros((2 * K, 128), F32)
    for j in range(K // 2):
        total = total + jnp.where(row == 2 * j + half, res[:, j * 128 : (j + 1) * 128], 0.0)
    total = total + swap(total)
    return jnp.where(low_lanes((K, 128)), total[:K], total[K:])


def mix_kernel(in_ref, w_ref, tables_ref, hat_ref, out_ref):
    spectra = x_analysis(in_ref, table(tables_ref, "x_in"))
    mixed = []
    for m in range(M):
        hat_ref[m] = spectra[m]
        mixed.append(mix(spectra[m], w_ref[m]))
    x_synthesis(mixed, table(tables_ref, "x_out"), out_ref)


def adjoint_kernel(in_ref, u_ref, w_ref, tables_ref, hats_ref, out_ref):
    spectra = x_analysis(in_ref, table(tables_ref, "x_in"))
    mixed = []
    for m in range(M):
        hats_ref[0, m] = u_ref[m]
        hats_ref[1, m] = spectra[m]
        mixed.append(mix_adjoint(spectra[m], w_ref[m]))
    x_synthesis(mixed, table(tables_ref, "x_out"), out_ref)


def grads_kernel(*refs):
    hats, (grads_out, grads, sems) = refs[:DP], refs[DP:]
    own = lax.broadcasted_iota(jnp.int32, (C, 2 * DP * K), 1) % K // 2
    odd = lax.broadcasted_iota(jnp.int32, (2 * DP * K, 1), 0) % 2 == 1
    copies = [pltpu.make_async_copy(grads.at[m], grads_out.at[m], sems.at[m]) for m in range(M)]
    for m in range(M):
        u, g = (jnp.concatenate([hat[i, m] for hat in hats], 0) for i in range(2))
        u_t = u.T.astype(BF)
        left = lanes([u_t[:C], u_t[C:]])
        right = jnp.concatenate([g, -turned(g)], 0)
        right = lanes([jnp.where(odd, 0.0, right), jnp.where(odd, right, 0.0)]).astype(BF)
        tall = jnp.concatenate([jnp.where(own == q, left, jnp.zeros_like(left)) for q in range(K // 2)], 0)
        out = dot(tall, right)
        for kx in range(K):
            grads[m, kx] = out[kx // 2 * C : (kx // 2 + 1) * C, kx % 2 * 128 : (kx % 2 + 1) * 128]
        copies[m].start()
    for copy in copies:
        copy.wait()


LIMIT = 32
IN_VMEM = pl.BlockSpec(memory_space=pltpu.VMEM)
IN_HBM = pl.BlockSpec(memory_space=pltpu.HBM)


def call(kernel, name, out_shapes, out_specs, scratch, *operands, specs):
    return pl.pallas_call(
        kernel,
        name=name,
        out_shape=out_shapes,
        in_specs=specs,
        out_specs=out_specs,
        scratch_shapes=scratch,
        compiler_params=pltpu.CompilerParams(vmem_limit_bytes=LIMIT * 2**20),
    )(*operands)


def in_vmem(*arrays):
    return [pltpu.with_memory_space_constraint(array, pltpu.VMEM) for array in arrays]


def in_hbm(*arrays):
    return [pltpu.with_memory_space_constraint(array, pltpu.HBM) for array in arrays]


def shape(dims, kind=F32):
    return jax.ShapeDtypeStruct(dims, kind)


SPECTRA = shape((SLABS, CX, M, 128))
BOTH_ROWS = pltpu.VMEM((CX, 2 * K, TP, 128), F32)
ROWS = pltpu.VMEM((2 * K, TP, 128), F32)


def exchange(data):
    return lax.all_to_all(data, "slab", 0, 0, tiled=True)


Y_RING = 4


def x_partner(data):
    return lax.ppermute(data, "dp", [(i, (i + Y_RING) % DP) for i in range(DP)])


def y_neighbours(data):
    return [
        lax.ppermute(data, "dp", [(i, i // Y_RING * Y_RING + (i + by) % Y_RING) for i in range(DP)])
        for by in (2, 3, 1)
    ]


def body(field, cotangent, mode_weights, w_local, bias):
    grid_shape = (CX, N, N * C)
    on_grid = pltpu.VMEM(grid_shape, BF)
    values, cot = field.reshape(grid_shape), cotangent.reshape(grid_shape)

    first, weights, tables, wide_map, wide_bias = call(
        analyse_kernel,
        "analyse",
        (
            SPECTRA,
            pltpu.VMEM((M, K * C, 2 * C), BF),
            pltpu.VMEM(PACKED.shape, BF),
            pltpu.VMEM((2 * C, 2 * C), BF),
            pltpu.VMEM((1, 2 * C), F32),
        ),
        [IN_VMEM] * 5,
        [on_grid, BOTH_ROWS, pltpu.VMEM((C, C), BF), pltpu.VMEM((1, C), F32), pltpu.SemaphoreType.DMA((8,))],
        *in_hbm(
            values, mode_weights.reshape(M, K * C, 2 * C), jnp.asarray(PACKED), w_local, bias.reshape(1, C)
        ),
        specs=[IN_HBM] * 5,
    )
    u_hat, mixed = call(
        mix_kernel,
        "mix",
        (shape((M, K, 128)), shape((N, M, 128))),
        [IN_VMEM] * 2,
        [],
        exchange(first).reshape(N, M, 128),
        *in_vmem(weights, tables),
        specs=[IN_VMEM] * 3,
    )
    arrived = exchange(mixed.reshape(SPECTRA.shape))
    gz, second = call(
        middle_kernel,
        "middle",
        (pltpu.HBM(grid_shape, BF), SPECTRA),
        [IN_HBM, IN_VMEM],
        [on_grid, BOTH_ROWS, BOTH_ROWS, pltpu.SemaphoreType.DMA((2,))],
        arrived,
        *in_vmem(values, cot, wide_map, wide_bias, tables),
        specs=[IN_VMEM] * 6,
    )
    hats, back = call(
        adjoint_kernel,
        "adjoint",
        (shape((2, M, K, 128)), shape((N, M, 128))),
        [IN_VMEM] * 2,
        [],
        exchange(second).reshape(N, M, 128),
        u_hat,
        *in_vmem(weights, tables),
        specs=[IN_VMEM] * 4,
    )
    partner = x_partner(hats)
    opposite, back_one, next_one = y_neighbours(hats)
    others = [opposite, back_one, next_one, partner, x_partner(opposite), *y_neighbours(partner)[1:]]
    grad_field = call(
        final_kernel,
        "final",
        pltpu.HBM(grid_shape, BF),
        IN_HBM,
        [on_grid, BOTH_ROWS, pltpu.SemaphoreType.DMA((2,))],
        exchange(back.reshape(SPECTRA.shape)),
        *in_vmem(gz, wide_map, tables),
        specs=[IN_VMEM] * 4,
    )
    grad_field, *others = lax.optimization_barrier((grad_field, *others))
    grad_modes = call(
        grads_kernel,
        "weight_grads",
        pltpu.HBM((M, K, C, 2 * C), F32),
        IN_HBM,
        [pltpu.VMEM((M, K, C, 2 * C), F32), pltpu.SemaphoreType.DMA((M,))],
        hats,
        *others,
        specs=[IN_VMEM] * DP,
    )
    return grad_field.reshape(field.shape), grad_modes


def solution(mesh):
    placed = (
        P("dp", "slab", None, None),
        P("dp", "slab", None, None),
        P("slab", None, None, None),
        P(),
        P(),
    )
    return jax.shard_map(
        body,
        mesh=mesh,
        in_specs=placed,
        out_specs=(P("dp", "slab", None, None), P("slab", None, None, None)),
        check_vma=False,
    )
```

```python
import math

import jax
import jax.numpy as jnp
import ml_dtypes
import numpy as np
from jax import lax
from jax.experimental import pallas as pl
from jax.experimental.pallas import tpu as pltpu
from jax.sharding import PartitionSpec as P

C = 64
K = 16
N = 64
CX = 2
SLABS = 32
DP = 8
TP = N // 2

BF = jnp.bfloat16
F32 = jnp.float32
SQRT_TWO_PI = math.sqrt(2.0 / math.pi)


def trig(freqs):
    phase = (freqs[:, None] * np.arange(N)[None, :] % N) * (2.0 * math.pi / N)
    return np.cos(phase) / math.sqrt(N), np.sin(phase) / math.sqrt(N)


def rounded(table):
    return table.astype(np.float32).astype(ml_dtypes.bfloat16)


def wide(table):
    high = rounded(table)
    low = rounded(table - high.astype(np.float64))
    return np.concatenate([high, low, high], 1)


def twice_table(table):
    high = rounded(table)
    low = rounded(table - high.astype(np.float64))
    return np.concatenate([high, low], 1)


SIGNED = np.concatenate([np.arange(K // 2), np.arange(-K // 2, 0)])
COS, SIN = trig(SIGNED)
T_COS, T_SIN = trig(np.arange(K))
P_RE, P_IM = T_COS.T, -T_SIN.T

Y_IN = twice_table(np.stack([COS, SIN], 1).reshape(2 * K, N))
Y_OUT = wide(np.concatenate([COS, SIN], 0).T)
X_IN = wide(np.concatenate([COS, SIN], 0))
X_OUT = wide(np.concatenate([COS, SIN], 0).T)


def t_in():
    re = rounded(P_RE).astype(np.float64).reshape(TP, 2, K)
    im = rounded(P_IM).astype(np.float64).reshape(TP, 2, K)
    rows_re = np.concatenate([re, im], 0)
    rows_im = np.concatenate([im, -re], 0)
    both = np.stack([rows_re, rows_im], 0)
    table = both.transpose(0, 2, 3, 1).reshape(4 * K, 2 * TP)
    return rounded(np.concatenate([table, table], 1))


def t_out():
    re = P_RE.reshape(TP, 2, K)
    im = P_IM.reshape(TP, 2, K)
    of_c = np.stack([re, im], 2)
    of_s = np.stack([im, -re], 2)
    return wide(np.concatenate([of_c, of_s], 0).reshape(2 * TP, 4 * K))


TABLES = {
    "y_in": Y_IN,
    "t_in": t_in(),
    "y_out": Y_OUT,
    "x_in": X_IN,
    "x_out": X_OUT,
    "t_out": t_out(),
}
PLACES = {}
for name, values in TABLES.items():
    PLACES[name] = (sum(TABLES[other].shape[0] for other in PLACES), *values.shape)
PACKED = np.concatenate([np.pad(v, ((0, 0), (0, 256 - v.shape[1]))) for v in TABLES.values()], 0)


def table(ref, name):
    first, rows, columns = PLACES[name]
    return ref[first : first + rows, :columns]


def dot(left, right):
    return jnp.dot(left, right, preferred_element_type=F32)


def split(data):
    high = data.astype(BF)
    return high, (data - high.astype(F32)).astype(BF)


def stack3(data):
    high, low = split(data)
    return jnp.concatenate([high, high, low], 0)


def stack2(data):
    high, low = split(data)
    return jnp.concatenate([high, low], 0)


def low_lanes(shape):
    return lax.broadcasted_iota(jnp.int32, shape, 1) < C


def swap(data):
    return pltpu.roll(data, C, 1)


def turned(data):
    other = swap(data)
    return jnp.where(low_lanes(data.shape), -other, other)


def lanes(blocks):
    return jnp.concatenate(blocks, 1)


Y_TILES = 32


def y_analysis_store(chunk, first_tile, tiles, y_in, scratch):
    out = dot(y_in, jnp.concatenate([chunk, chunk], 0))
    scratch[:, first_tile : first_tile + tiles, :] = out.reshape(2 * K, tiles, 128)


def t_analysis(scratch, t_table, out_ref, x, group=16):
    low = low_lanes((K, 128))
    for first in range(0, K, group):
        data = lanes([scratch[2 * (first + j) : 2 * (first + j + 1)].reshape(2 * TP, 128) for j in range(group)])
        res = dot(t_table, stack2(data))
        for j in range(group):
            re0, re1, im0, im1 = (res[q * K : (q + 1) * K, j * 128 : (j + 1) * 128] for q in range(4))
            both = jnp.where(low, re0, im1) + swap(jnp.where(low, im0, re1))
            out_ref[2 * (first + j), x] = both[:8]
            out_ref[2 * (first + j) + 1, x] = both[8:]


def t_synthesis(w_ref, t_table, scratch, x, group=16):
    low = low_lanes((K, 128))
    zero = jnp.zeros((K, 128), F32)
    for first in range(0, K, group):
        blocks = []
        for j in range(group):
            w = jnp.concatenate([w_ref[2 * (first + j), x], w_ref[2 * (first + j) + 1, x]], 0)
            other = swap(w)
            blocks.append(
                jnp.concatenate(
                    [
                        jnp.where(low, w, zero),
                        jnp.where(low, other, zero),
                        jnp.where(low, zero, other),
                        jnp.where(low, zero, w),
                    ],
                    0,
                )
            )
        res = dot(t_table, stack3(lanes(blocks)))
        for cs in range(2):
            scratch[:, cs * K + first : cs * K + first + group, :] = res[cs * TP : (cs + 1) * TP].reshape(
                TP, group, 128
            )


def y_synthesis(scratch, first_tile, tiles, y_out):
    data = lanes(
        [
            scratch[first_tile + j]
            for j in range(tiles)
        ]
    )
    return dot(y_out, stack3(data))


def channel_map(chunk, weight, tiles, contracted=0):
    rows = jnp.concatenate([chunk[:, j * 128 : (j + 1) * 128] for j in range(tiles)], 0)
    out = lax.dot_general(
        rows, weight, (((1,), (contracted,)), ((), ())), preferred_element_type=F32
    )
    return lanes([out[j * N : (j + 1) * N] for j in range(tiles)])


def lane_slice(step, tiles):
    return pl.ds(step * tiles * 128, tiles * 128)


HALF = N * C // 2


def start_all(sems, *moves):
    copies = [pltpu.make_async_copy(*move, sems.at[i]) for i, move in enumerate(moves)]
    for copy in copies:
        copy.start()
    return copies


def analyse_kernel(
    field_in, w_in, tables_in, map_in, bias_in,
    out_ref, w_ref, tables_ref, map_ref, bias_ref,
    field, scratch, small_map, small_bias, sems,
):
    parts = [(i // 2, slice(None), pl.ds(i % 2 * HALF, HALF)) for i in range(2 * CX)]
    copies = start_all(
        sems,
        (tables_in, tables_ref),
        *((field_in.at[part], field.at[part]) for part in parts),
        (map_in, small_map),
        (bias_in, small_bias),
        (w_in, w_ref),
    )
    copies[0].wait()
    y_in, t_in = table(tables_ref, "y_in"), table(tables_ref, "t_in")
    for x in range(CX):
        copies[1 + 2 * x].wait()
        copies[2 + 2 * x].wait()
        y_analysis_store(field[x], 0, TP, y_in, scratch.at[x])
    for x in range(CX):
        t_analysis(scratch.at[x], t_in, out_ref, x)
    for copy in copies[1 + 2 * CX :]:
        copy.wait()
    wide_map = jnp.concatenate([small_map[...]] * 2, 1)
    wide_map = jnp.concatenate([wide_map] * 2, 0)
    row = lax.broadcasted_iota(jnp.int32, (2 * C, 2 * C), 0) // C
    lane = lax.broadcasted_iota(jnp.int32, (2 * C, 2 * C), 1) // C
    map_ref[...] = jnp.where(row == lane, wide_map, jnp.zeros_like(wide_map))
    bias_ref[...] = jnp.concatenate([small_bias[...]] * 2, 1)


def gelu_slope(z):
    square = z * z
    tanh_value = jnp.tanh(z * (SQRT_TWO_PI + SQRT_TWO_PI * 0.044715 * square))
    half_rise = z * (0.5 * SQRT_TWO_PI + 1.5 * SQRT_TWO_PI * 0.044715 * square)
    return (1.0 + tanh_value) * (0.5 + half_rise * (1.0 - tanh_value))


def middle_kernel(
    w_ref, field, cot, map_ref, bias_ref, tables_ref, gz_out, out_ref, gz, syn, ana, sems
):
    backs = [pltpu.make_async_copy(gz.at[x], gz_out.at[x], sems.at[x]) for x in range(CX)]
    y_in, y_out, t_in, t_out = (table(tables_ref, name) for name in ("y_in", "y_out", "t_in", "t_out"))
    for x in range(CX):
        t_synthesis(w_ref, t_out, syn.at[x], x)
    for x in range(CX):

        for step in range(TP // Y_TILES):
            at = lane_slice(step, Y_TILES)
            spec = y_synthesis(syn.at[x], step * Y_TILES, Y_TILES, y_out)
            z = spec + channel_map(field[x, :, at], map_ref[...], Y_TILES) + lanes([bias_ref[...]] * Y_TILES)
            out = (cot[x, :, at].astype(F32) * gelu_slope(z)).astype(BF)
            gz[x, :, at] = out
            y_analysis_store(out, step * Y_TILES, Y_TILES, y_in, ana.at[x])

        backs[x].start()
    for x in range(CX):
        t_analysis(ana.at[x], t_in, out_ref, x)
    for back in backs:
        back.wait()


def final_kernel(w_ref, gz, map_ref, tables_ref, grad_out, grad, syn, sems):
    backs = [pltpu.make_async_copy(grad.at[x], grad_out.at[x], sems.at[x]) for x in range(CX)]
    y_out, t_out = table(tables_ref, "y_out"), table(tables_ref, "t_out")
    for x in range(CX):
        t_synthesis(w_ref, t_out, syn.at[x], x)
    for x in range(CX):

        for step in range(TP // Y_TILES):
            at = lane_slice(step, Y_TILES)
            spec = y_synthesis(syn.at[x], step * Y_TILES, Y_TILES, y_out)
            grad[x, :, at] = (spec + channel_map(gz[x, :, at], map_ref[...], Y_TILES, 1)).astype(BF)

        backs[x].start()
    return backs


M = 8


def x_analysis(in_ref, x_in):
    data = in_ref[...].reshape(N, M * 128)
    res = dot(x_in, stack3(data))
    out = []
    for m in range(M):
        cos_part = res[:K, m * 128 : (m + 1) * 128]
        sin_part = res[K:, m * 128 : (m + 1) * 128]
        out.append(cos_part - turned(sin_part))
    return out


def x_synthesis(blocks, x_out, out_ref):
    data = lanes([jnp.concatenate([v, turned(v)], 0) for v in blocks])
    res = dot(x_out, stack3(data))
    out_ref[...] = res.reshape(N, M, 128)


def mix(u, weights):
    low = low_lanes((K, 128))
    other = swap(u)
    rows = jnp.concatenate([jnp.where(low, u, other), jnp.where(low, other, u)], 0)
    parts = jnp.concatenate(split(rows), 0).astype(F32)
    row = lax.broadcasted_iota(jnp.int32, (4 * K, 128), 0) % K
    half = lax.broadcasted_iota(jnp.int32, (4 * K, 128), 1) // C
    left = lanes([jnp.where(row == 2 * j + half, parts, 0.0).astype(BF) for j in range(K // 2)])
    res = dot(left, weights)
    res = res[: 2 * K] + res[2 * K :]
    return res[:K] + turned(res[K:])


def mix_adjoint(g, weights):
    rows = jnp.concatenate([g, -turned(g)], 0)
    parts = jnp.concatenate(split(rows), 0)
    res = lax.dot_general(parts, weights, (((1,), (1,)), ((), ())), preferred_element_type=F32)
    res = res[: 2 * K] + res[2 * K :]
    row = lax.broadcasted_iota(jnp.int32, (2 * K, 128), 0) % K
    half = lax.broadcasted_iota(jnp.int32, (2 * K, 128), 1) // C
    total = jnp.zeros((2 * K, 128), F32)
    for j in range(K // 2):
        total = total + jnp.where(row == 2 * j + half, res[:, j * 128 : (j + 1) * 128], 0.0)
    total = total + swap(total)
    return jnp.where(low_lanes((K, 128)), total[:K], total[K:])


def mix_kernel(in_ref, w_ref, tables_ref, hat_ref, out_ref):
    spectra = x_analysis(in_ref, table(tables_ref, "x_in"))
    mixed = []
    for m in range(M):
        hat_ref[m] = spectra[m]
        mixed.append(mix(spectra[m], w_ref[m]))
    x_synthesis(mixed, table(tables_ref, "x_out"), out_ref)


def adjoint_kernel(in_ref, u_ref, w_ref, tables_ref, hats_ref, out_ref):
    spectra = x_analysis(in_ref, table(tables_ref, "x_in"))
    mixed = []
    for m in range(M):
        hats_ref[0, m] = u_ref[m]
        hats_ref[1, m] = spectra[m]
        mixed.append(mix_adjoint(spectra[m], w_ref[m]))
    x_synthesis(mixed, table(tables_ref, "x_out"), out_ref)


def grads_kernel(*refs):
    hats, (grads_out, grads, sems) = refs[:DP], refs[DP:]
    own = lax.broadcasted_iota(jnp.int32, (C, 2 * DP * K), 1) % K // 2
    odd = lax.broadcasted_iota(jnp.int32, (2 * DP * K, 1), 0) % 2 == 1
    copies = [pltpu.make_async_copy(grads.at[m], grads_out.at[m], sems.at[m]) for m in range(M)]
    for m in range(M):
        u, g = (jnp.concatenate([hat[i, m] for hat in hats], 0) for i in range(2))
        u_t = u.T.astype(BF)
        left = lanes([u_t[:C], u_t[C:]])
        right = jnp.concatenate([g, -turned(g)], 0)
        right = lanes([jnp.where(odd, 0.0, right), jnp.where(odd, right, 0.0)]).astype(BF)
        tall = jnp.concatenate([jnp.where(own == q, left, jnp.zeros_like(left)) for q in range(K // 2)], 0)
        out = dot(tall, right)
        for kx in range(K):
            grads[m, kx] = out[kx // 2 * C : (kx // 2 + 1) * C, kx % 2 * 128 : (kx % 2 + 1) * 128]
        copies[m].start()
    return copies


def finish_kernel(w_ref, gz, map_ref, tables_ref, *refs):
    hats, (grad_out, modes_out, grad, syn, modes, sems, mode_sems) = refs[:DP], refs[DP:]
    written = grads_kernel(*hats, modes_out, modes, mode_sems)
    written += final_kernel(w_ref, gz, map_ref, tables_ref, grad_out, grad, syn, sems)
    for copy in written:
        copy.wait()


LIMIT = 32
IN_VMEM = pl.BlockSpec(memory_space=pltpu.VMEM)
IN_HBM = pl.BlockSpec(memory_space=pltpu.HBM)


def call(kernel, name, out_shapes, out_specs, scratch, *operands, specs):
    return pl.pallas_call(
        kernel,
        name=name,
        out_shape=out_shapes,
        in_specs=specs,
        out_specs=out_specs,
        scratch_shapes=scratch,
        compiler_params=pltpu.CompilerParams(vmem_limit_bytes=LIMIT * 2**20),
    )(*operands)


def in_vmem(*arrays):
    return [pltpu.with_memory_space_constraint(array, pltpu.VMEM) for array in arrays]


def in_hbm(*arrays):
    return [pltpu.with_memory_space_constraint(array, pltpu.HBM) for array in arrays]


def shape(dims, kind=F32):
    return jax.ShapeDtypeStruct(dims, kind)


SPECTRA = shape((SLABS, CX, M, 128))
BOTH_ROWS = pltpu.VMEM((CX, 2 * K, TP, 128), F32)
ROWS = pltpu.VMEM((2 * K, TP, 128), F32)


def exchange(data):
    return lax.all_to_all(data, "slab", 0, 0, tiled=True)


Y_RING = 4


def x_partner(data):
    return lax.ppermute(data, "dp", [(i, (i + Y_RING) % DP) for i in range(DP)])


def y_neighbours(data):
    return [
        lax.ppermute(data, "dp", [(i, i ^ by) for i in range(DP)])
        for by in (2, 1, 3)
    ]


def body(field, cotangent, mode_weights, w_local, bias):
    grid_shape = (CX, N, N * C)
    on_grid = pltpu.VMEM(grid_shape, BF)
    values, cot = field.reshape(grid_shape), cotangent.reshape(grid_shape)

    first, weights, tables, wide_map, wide_bias = call(
        analyse_kernel,
        "analyse",
        (
            SPECTRA,
            pltpu.VMEM((M, K * C, 2 * C), BF),
            pltpu.VMEM(PACKED.shape, BF),
            pltpu.VMEM((2 * C, 2 * C), BF),
            pltpu.VMEM((1, 2 * C), F32),
        ),
        [IN_VMEM] * 5,
        [on_grid, BOTH_ROWS, pltpu.VMEM((C, C), BF), pltpu.VMEM((1, C), F32), pltpu.SemaphoreType.DMA((8,))],
        *in_hbm(
            values, mode_weights.reshape(M, K * C, 2 * C), jnp.asarray(PACKED), w_local, bias.reshape(1, C)
        ),
        specs=[IN_HBM] * 5,
    )
    u_hat, mixed = call(
        mix_kernel,
        "mix",
        (shape((M, K, 128)), shape((N, M, 128))),
        [IN_VMEM] * 2,
        [],
        exchange(first).reshape(N, M, 128),
        *in_vmem(weights, tables),
        specs=[IN_VMEM] * 3,
    )
    arrived = exchange(mixed.reshape(SPECTRA.shape))
    gz, second = call(
        middle_kernel,
        "middle",
        (pltpu.HBM(grid_shape, BF), SPECTRA),
        [IN_HBM, IN_VMEM],
        [on_grid, BOTH_ROWS, BOTH_ROWS, pltpu.SemaphoreType.DMA((2,))],
        arrived,
        *in_vmem(values, cot, wide_map, wide_bias, tables),
        specs=[IN_VMEM] * 6,
    )
    hats, back = call(
        adjoint_kernel,
        "adjoint",
        (shape((2, M, K, 128)), shape((N, M, 128))),
        [IN_VMEM] * 2,
        [],
        exchange(second).reshape(N, M, 128),
        u_hat,
        *in_vmem(weights, tables),
        specs=[IN_VMEM] * 4,
    )
    partner = x_partner(hats)
    opposite, back_one, next_one = y_neighbours(hats)
    others = [opposite, back_one, next_one, partner, x_partner(opposite), *y_neighbours(partner)[1:]]
    grad_field, grad_modes = call(
        finish_kernel,
        "finish",
        (pltpu.HBM(grid_shape, BF), pltpu.HBM((M, K, C, 2 * C), F32)),
        [IN_HBM] * 2,
        [
            on_grid,
            BOTH_ROWS,
            pltpu.VMEM((M, K, C, 2 * C), F32),
            pltpu.SemaphoreType.DMA((CX,)),
            pltpu.SemaphoreType.DMA((M,)),
        ],
        exchange(back.reshape(SPECTRA.shape)),
        *in_vmem(gz, wide_map, tables),
        hats,
        *others,
        specs=[IN_VMEM] * (4 + DP),
    )
    return grad_field.reshape(field.shape), grad_modes


def solution(mesh):
    placed = (
        P("dp", "slab", None, None),
        P("dp", "slab", None, None),
        P("slab", None, None, None),
        P(),
        P(),
    )
    return jax.shard_map(
        body,
        mesh=mesh,
        in_specs=placed,
        out_specs=(P("dp", "slab", None, None), P("slab", None, None, None)),
        check_vma=False,
    )
```

```python
import math

import jax
import jax.numpy as jnp
import ml_dtypes
import numpy as np
from jax import lax
from jax.experimental import pallas as pl
from jax.experimental.pallas import tpu as pltpu
from jax.sharding import PartitionSpec as P

C = 64
K = 16
N = 64
CX = 2
SLABS = 32
DP = 8
TP = N // 2

BF = jnp.bfloat16
F32 = jnp.float32
SQRT_TWO_PI = math.sqrt(2.0 / math.pi)


def trig(freqs):
    phase = (freqs[:, None] * np.arange(N)[None, :] % N) * (2.0 * math.pi / N)
    return np.cos(phase) / math.sqrt(N), np.sin(phase) / math.sqrt(N)


def rounded(table):
    return table.astype(np.float32).astype(ml_dtypes.bfloat16)


def wide(table):
    high = rounded(table)
    low = rounded(table - high.astype(np.float64))
    return np.concatenate([high, low, high], 1)


def twice_table(table):
    high = rounded(table)
    low = rounded(table - high.astype(np.float64))
    return np.concatenate([high, low], 1)


SIGNED = np.concatenate([np.arange(K // 2), np.arange(-K // 2, 0)])
COS, SIN = trig(SIGNED)
T_COS, T_SIN = trig(np.arange(K))
P_RE, P_IM = T_COS.T, -T_SIN.T

Y_IN = twice_table(np.stack([COS, SIN], 1).reshape(2 * K, N))
Y_OUT = wide(np.concatenate([COS, SIN], 0).T)
X_IN = wide(np.concatenate([COS, SIN], 0))
X_OUT = wide(np.concatenate([COS, SIN], 0).T)


def t_in():
    re = rounded(P_RE).astype(np.float64).reshape(TP, 2, K)
    im = rounded(P_IM).astype(np.float64).reshape(TP, 2, K)
    rows_re = np.concatenate([re, im], 0)
    rows_im = np.concatenate([im, -re], 0)
    both = np.stack([rows_re, rows_im], 0)
    table = both.transpose(0, 2, 3, 1).reshape(4 * K, 2 * TP)
    return rounded(np.concatenate([table, table], 1))


def t_out():
    re = P_RE.reshape(TP, 2, K)
    im = P_IM.reshape(TP, 2, K)
    of_c = np.stack([re, im], 2)
    of_s = np.stack([im, -re], 2)
    return wide(np.concatenate([of_c, of_s], 0).reshape(2 * TP, 4 * K))


TABLES = {
    "y_in": Y_IN,
    "t_in": t_in(),
    "y_out": Y_OUT,
    "x_in": X_IN,
    "x_out": X_OUT,
    "t_out": t_out(),
}
PLACES = {}
for name, values in TABLES.items():
    PLACES[name] = (sum(TABLES[other].shape[0] for other in PLACES), *values.shape)
PACKED = np.concatenate([np.pad(v, ((0, 0), (0, 256 - v.shape[1]))) for v in TABLES.values()], 0)


def table(ref, name):
    first, rows, columns = PLACES[name]
    return ref[first : first + rows, :columns]


def dot(left, right):
    return jnp.dot(left, right, preferred_element_type=F32)


def split(data):
    high = data.astype(BF)
    return high, (data - high.astype(F32)).astype(BF)


def stack3(data):
    high, low = split(data)
    return jnp.concatenate([high, high, low], 0)


def stack2(data):
    high, low = split(data)
    return jnp.concatenate([high, low], 0)


def low_lanes(shape):
    return lax.broadcasted_iota(jnp.int32, shape, 1) < C


def swap(data):
    return pltpu.roll(data, C, 1)


def turned(data):
    other = swap(data)
    return jnp.where(low_lanes(data.shape), -other, other)


def lanes(blocks):
    return jnp.concatenate(blocks, 1)


Y_TILES = 32


def y_analysis_store(chunk, first_tile, tiles, y_in, scratch):
    out = dot(y_in, jnp.concatenate([chunk, chunk], 0))
    scratch[:, first_tile : first_tile + tiles, :] = out.reshape(2 * K, tiles, 128)


def t_analysis(scratch, t_table, out_ref, x, group=16):
    low = low_lanes((K, 128))
    for first in range(0, K, group):
        data = lanes([scratch[2 * (first + j) : 2 * (first + j + 1)].reshape(2 * TP, 128) for j in range(group)])
        res = dot(t_table, stack2(data))
        for j in range(group):
            re0, re1, im0, im1 = (res[q * K : (q + 1) * K, j * 128 : (j + 1) * 128] for q in range(4))
            both = jnp.where(low, re0, im1) + swap(jnp.where(low, im0, re1))
            out_ref[2 * (first + j), x] = both[:8]
            out_ref[2 * (first + j) + 1, x] = both[8:]


def t_synthesis(w_ref, t_table, scratch, x, group=16):
    low = low_lanes((K, 128))
    zero = jnp.zeros((K, 128), F32)
    for first in range(0, K, group):
        blocks = []
        for j in range(group):
            w = jnp.concatenate([w_ref[2 * (first + j), x], w_ref[2 * (first + j) + 1, x]], 0)
            other = swap(w)
            blocks.append(
                jnp.concatenate(
                    [
                        jnp.where(low, w, zero),
                        jnp.where(low, other, zero),
                        jnp.where(low, zero, other),
                        jnp.where(low, zero, w),
                    ],
                    0,
                )
            )
        res = dot(t_table, stack3(lanes(blocks)))
        for cs in range(2):
            scratch[:, cs * K + first : cs * K + first + group, :] = res[cs * TP : (cs + 1) * TP].reshape(
                TP, group, 128
            )


def y_synthesis(scratch, first_tile, tiles, y_out):
    data = lanes(
        [
            scratch[first_tile + j]
            for j in range(tiles)
        ]
    )
    return dot(y_out, stack3(data))


def channel_map(chunk, weight, tiles, contracted=0):
    rows = jnp.concatenate([chunk[:, j * 128 : (j + 1) * 128] for j in range(tiles)], 0)
    out = lax.dot_general(
        rows, weight, (((1,), (contracted,)), ((), ())), preferred_element_type=F32
    )
    return lanes([out[j * N : (j + 1) * N] for j in range(tiles)])


def lane_slice(step, tiles):
    return pl.ds(step * tiles * 128, tiles * 128)


HALF = N * C // 2


def start_all(sems, *moves):
    copies = [pltpu.make_async_copy(*move, sems.at[i]) for i, move in enumerate(moves)]
    for copy in copies:
        copy.start()
    return copies


def analyse_kernel(
    field_in, w_in, tables_in, map_in, bias_in,
    out_ref, w_ref, tables_ref, map_ref, bias_ref,
    field, scratch, small_map, small_bias, sems,
):
    parts = [(i // 2, slice(None), pl.ds(i % 2 * HALF, HALF)) for i in range(2 * CX)]
    copies = start_all(
        sems,
        (tables_in, tables_ref),
        *((field_in.at[part], field.at[part]) for part in parts),
        (map_in, small_map),
        (bias_in, small_bias),
        (w_in, w_ref),
    )
    copies[0].wait()
    y_in, t_in = table(tables_ref, "y_in"), table(tables_ref, "t_in")
    for x in range(CX):
        copies[1 + 2 * x].wait()
        copies[2 + 2 * x].wait()
        y_analysis_store(field[x], 0, TP, y_in, scratch.at[x])
    for x in range(CX):
        t_analysis(scratch.at[x], t_in, out_ref, x)
    for copy in copies[1 + 2 * CX :]:
        copy.wait()
    wide_map = jnp.concatenate([small_map[...]] * 2, 1)
    wide_map = jnp.concatenate([wide_map] * 2, 0)
    row = lax.broadcasted_iota(jnp.int32, (2 * C, 2 * C), 0) // C
    lane = lax.broadcasted_iota(jnp.int32, (2 * C, 2 * C), 1) // C
    map_ref[...] = jnp.where(row == lane, wide_map, jnp.zeros_like(wide_map))
    bias_ref[...] = jnp.concatenate([small_bias[...]] * 2, 1)


def gelu_slope(z):
    square = z * z
    tanh_value = jnp.tanh(z * (SQRT_TWO_PI + SQRT_TWO_PI * 0.044715 * square))
    half_rise = z * (0.5 * SQRT_TWO_PI + 1.5 * SQRT_TWO_PI * 0.044715 * square)
    return (1.0 + tanh_value) * (0.5 + half_rise * (1.0 - tanh_value))


def middle_kernel(
    w_ref, field, cot, map_ref, bias_ref, tables_ref, gz_out, out_ref, gz, syn, ana, sems
):
    backs = [pltpu.make_async_copy(gz.at[x], gz_out.at[x], sems.at[x]) for x in range(CX)]
    y_in, y_out, t_in, t_out = (table(tables_ref, name) for name in ("y_in", "y_out", "t_in", "t_out"))
    for x in range(CX):
        t_synthesis(w_ref, t_out, syn.at[x], x)
    for x in range(CX):

        for step in range(TP // Y_TILES):
            at = lane_slice(step, Y_TILES)
            spec = y_synthesis(syn.at[x], step * Y_TILES, Y_TILES, y_out)
            z = spec + channel_map(field[x, :, at], map_ref[...], Y_TILES) + lanes([bias_ref[...]] * Y_TILES)
            out = (cot[x, :, at].astype(F32) * gelu_slope(z)).astype(BF)
            gz[x, :, at] = out
            y_analysis_store(out, step * Y_TILES, Y_TILES, y_in, ana.at[x])

        backs[x].start()
    for x in range(CX):
        t_analysis(ana.at[x], t_in, out_ref, x)
    for back in backs:
        back.wait()


def final_kernel(w_ref, gz, map_ref, tables_ref, grad_out, grad, syn, sems):
    backs = [pltpu.make_async_copy(grad.at[x], grad_out.at[x], sems.at[x]) for x in range(CX)]
    y_out, t_out = table(tables_ref, "y_out"), table(tables_ref, "t_out")
    for x in range(CX):
        t_synthesis(w_ref, t_out, syn.at[x], x)
    for x in range(CX):

        for step in range(TP // Y_TILES):
            at = lane_slice(step, Y_TILES)
            spec = y_synthesis(syn.at[x], step * Y_TILES, Y_TILES, y_out)
            grad[x, :, at] = (spec + channel_map(gz[x, :, at], map_ref[...], Y_TILES, 1)).astype(BF)

        backs[x].start()
    return backs


M = 8


def x_analysis(in_ref, x_in):
    data = in_ref[...].reshape(N, M * 128)
    res = dot(x_in, stack3(data))
    out = []
    for m in range(M):
        cos_part = res[:K, m * 128 : (m + 1) * 128]
        sin_part = res[K:, m * 128 : (m + 1) * 128]
        out.append(cos_part - turned(sin_part))
    return out


def x_synthesis(blocks, x_out, out_ref):
    data = lanes([jnp.concatenate([v, turned(v)], 0) for v in blocks])
    res = dot(x_out, stack3(data))
    out_ref[...] = res.reshape(N, M, 128)


def mix(u, weights):
    low = low_lanes((K, 128))
    other = swap(u)
    rows = jnp.concatenate([jnp.where(low, u, other), jnp.where(low, other, u)], 0)
    parts = jnp.concatenate(split(rows), 0)
    row = lax.broadcasted_iota(jnp.int32, (4 * K, 128), 0) % K
    half = lax.broadcasted_iota(jnp.int32, (4 * K, 128), 1) // C
    left = lanes([jnp.where(row == 2 * j + half, parts, jnp.zeros_like(parts)) for j in range(K // 2)])
    res = dot(left, weights)
    res = res[: 2 * K] + res[2 * K :]
    return res[:K] + turned(res[K:])


def mix_adjoint(g, weights):
    rows = jnp.concatenate([g, -turned(g)], 0)
    parts = jnp.concatenate(split(rows), 0)
    res = lax.dot_general(parts, weights, (((1,), (1,)), ((), ())), preferred_element_type=F32)
    res = res[: 2 * K] + res[2 * K :]
    row = lax.broadcasted_iota(jnp.int32, (2 * K, 128), 0) % K
    half = lax.broadcasted_iota(jnp.int32, (2 * K, 128), 1) // C
    total = jnp.zeros((2 * K, 128), F32)
    for j in range(K // 2):
        total = total + jnp.where(row == 2 * j + half, res[:, j * 128 : (j + 1) * 128], 0.0)
    total = total + swap(total)
    return jnp.where(low_lanes((K, 128)), total[:K], total[K:])


def mix_kernel(in_ref, w_ref, tables_ref, hat_ref, out_ref):
    spectra = x_analysis(in_ref, table(tables_ref, "x_in"))
    mixed = []
    for m in range(M):
        hat_ref[m] = spectra[m]
        mixed.append(mix(spectra[m], w_ref[m]))
    x_synthesis(mixed, table(tables_ref, "x_out"), out_ref)


def adjoint_kernel(in_ref, u_ref, w_ref, tables_ref, hats_ref, out_ref):
    spectra = x_analysis(in_ref, table(tables_ref, "x_in"))
    mixed = []
    for m in range(M):
        hats_ref[0, m] = u_ref[m]
        hats_ref[1, m] = spectra[m]
        mixed.append(mix_adjoint(spectra[m], w_ref[m]))
    x_synthesis(mixed, table(tables_ref, "x_out"), out_ref)


def grads_kernel(*refs):
    hats, (grads_out, grads, sems) = refs[:DP], refs[DP:]
    own = lax.broadcasted_iota(jnp.int32, (C, 2 * DP * K), 1) % K // 2
    odd = lax.broadcasted_iota(jnp.int32, (2 * DP * K, 1), 0) % 2 == 1
    copies = [pltpu.make_async_copy(grads.at[m], grads_out.at[m], sems.at[m]) for m in range(M)]
    for m in range(M):
        u, g = (jnp.concatenate([hat[i, m] for hat in hats], 0) for i in range(2))
        u_t = u.T.astype(BF)
        left = lanes([u_t[:C], u_t[C:]])
        right = jnp.concatenate([g, -turned(g)], 0)
        right = lanes([jnp.where(odd, 0.0, right), jnp.where(odd, right, 0.0)]).astype(BF)
        tall = jnp.concatenate([jnp.where(own == q, left, jnp.zeros_like(left)) for q in range(K // 2)], 0)
        out = dot(tall, right)
        for kx in range(K):
            grads[m, kx] = out[kx // 2 * C : (kx // 2 + 1) * C, kx % 2 * 128 : (kx % 2 + 1) * 128]
        copies[m].start()
    return copies


def finish_kernel(w_ref, gz, map_ref, tables_ref, *refs):
    hats, (grad_out, modes_out, grad, syn, modes, sems, mode_sems) = refs[:DP], refs[DP:]
    written = grads_kernel(*hats, modes_out, modes, mode_sems)
    written += final_kernel(w_ref, gz, map_ref, tables_ref, grad_out, grad, syn, sems)
    for copy in written:
        copy.wait()


LIMIT = 32
IN_VMEM = pl.BlockSpec(memory_space=pltpu.VMEM)
IN_HBM = pl.BlockSpec(memory_space=pltpu.HBM)


def call(kernel, name, out_shapes, out_specs, scratch, *operands, specs):
    return pl.pallas_call(
        kernel,
        name=name,
        out_shape=out_shapes,
        in_specs=specs,
        out_specs=out_specs,
        scratch_shapes=scratch,
        compiler_params=pltpu.CompilerParams(vmem_limit_bytes=LIMIT * 2**20),
    )(*operands)


def in_vmem(*arrays):
    return [pltpu.with_memory_space_constraint(array, pltpu.VMEM) for array in arrays]


def in_hbm(*arrays):
    return [pltpu.with_memory_space_constraint(array, pltpu.HBM) for array in arrays]


def shape(dims, kind=F32):
    return jax.ShapeDtypeStruct(dims, kind)


SPECTRA = shape((SLABS, CX, M, 128))
BOTH_ROWS = pltpu.VMEM((CX, 2 * K, TP, 128), F32)
ROWS = pltpu.VMEM((2 * K, TP, 128), F32)


def exchange(data):
    return lax.all_to_all(data, "slab", 0, 0, tiled=True)


Y_RING = 4


def x_partner(data):
    return lax.ppermute(data, "dp", [(i, (i + Y_RING) % DP) for i in range(DP)])


def y_neighbours(data):
    return [
        lax.ppermute(data, "dp", [(i, i ^ by) for i in range(DP)])
        for by in (2, 1, 3)
    ]


def body(field, cotangent, mode_weights, w_local, bias):
    grid_shape = (CX, N, N * C)
    on_grid = pltpu.VMEM(grid_shape, BF)
    values, cot = field.reshape(grid_shape), cotangent.reshape(grid_shape)

    first, weights, tables, wide_map, wide_bias = call(
        analyse_kernel,
        "analyse",
        (
            SPECTRA,
            pltpu.VMEM((M, K * C, 2 * C), BF),
            pltpu.VMEM(PACKED.shape, BF),
            pltpu.VMEM((2 * C, 2 * C), BF),
            pltpu.VMEM((1, 2 * C), F32),
        ),
        [IN_VMEM] * 5,
        [on_grid, BOTH_ROWS, pltpu.VMEM((C, C), BF), pltpu.VMEM((1, C), F32), pltpu.SemaphoreType.DMA((8,))],
        *in_hbm(
            values, mode_weights.reshape(M, K * C, 2 * C), jnp.asarray(PACKED), w_local, bias.reshape(1, C)
        ),
        specs=[IN_HBM] * 5,
    )
    u_hat, mixed = call(
        mix_kernel,
        "mix",
        (shape((M, K, 128)), shape((N, M, 128))),
        [IN_VMEM] * 2,
        [],
        exchange(first).reshape(N, M, 128),
        *in_vmem(weights, tables),
        specs=[IN_VMEM] * 3,
    )
    arrived = exchange(mixed.reshape(SPECTRA.shape))
    gz, second = call(
        middle_kernel,
        "middle",
        (pltpu.HBM(grid_shape, BF), SPECTRA),
        [IN_HBM, IN_VMEM],
        [on_grid, BOTH_ROWS, BOTH_ROWS, pltpu.SemaphoreType.DMA((2,))],
        arrived,
        *in_vmem(values, cot, wide_map, wide_bias, tables),
        specs=[IN_VMEM] * 6,
    )
    hats, back = call(
        adjoint_kernel,
        "adjoint",
        (shape((2, M, K, 128)), shape((N, M, 128))),
        [IN_VMEM] * 2,
        [],
        exchange(second).reshape(N, M, 128),
        u_hat,
        *in_vmem(weights, tables),
        specs=[IN_VMEM] * 4,
    )
    partner = x_partner(hats)
    opposite, back_one, next_one = y_neighbours(hats)
    others = [opposite, back_one, next_one, partner, x_partner(opposite), *y_neighbours(partner)[1:]]
    grad_field, grad_modes = call(
        finish_kernel,
        "finish",
        (pltpu.HBM(grid_shape, BF), pltpu.HBM((M, K, C, 2 * C), F32)),
        [IN_HBM] * 2,
        [
            on_grid,
            BOTH_ROWS,
            pltpu.VMEM((M, K, C, 2 * C), F32),
            pltpu.SemaphoreType.DMA((CX,)),
            pltpu.SemaphoreType.DMA((M,)),
        ],
        exchange(back.reshape(SPECTRA.shape)),
        *in_vmem(gz, wide_map, tables),
        hats,
        *others,
        specs=[IN_VMEM] * (4 + DP),
    )
    return grad_field.reshape(field.shape), grad_modes


def solution(mesh):
    placed = (
        P("dp", "slab", None, None),
        P("dp", "slab", None, None),
        P("slab", None, None, None),
        P(),
        P(),
    )
    return jax.shard_map(
        body,
        mesh=mesh,
        in_specs=placed,
        out_specs=(P("dp", "slab", None, None), P("slab", None, None, None)),
        check_vma=False,
    )
```
